32 devices in a mesh: hx: 8 (over y, x, core), nb: 4 (over z).
Axes of the slice: x: 2, y: 2, z: 4, core: 2. Of those that a mesh axis runs over, the one named last changes fastest.
Arguments:
- partial_multipoles: bfloat16 [4, 4096, 1464], P('nb', 'hx'), may hold values from -6 to 6
- shared_slots: int32 [4, 4096], P('nb', 'hx'), may hold values from -1 to 1023, as said below
- m2l_sources: int32 [4, 2, 8192], P('nb', None, 'hx'), may hold values from 0 to 1023
- m2l_ops: bfloat16 [2, 1464, 1464], replicated, may hold values from -0.15625 to 0.15625
- positions: float32 [4, 3, 16384], P('nb', None, 'hx'), may hold values from -1 to 1
- forces: float32 [4, 3, 16384], P('nb', None, 'hx'), may hold values from -6 to 6
- leaf_counts: int32 [4, 128], P('nb', 'hx'), may hold values from 32 to 128
- neighbours: int32 [4, 8, 128], P('nb', None, 'hx'), may hold values from 0 to 47
Outputs:
- local_expansion: bfloat16 [4, 8192, 1464], P('nb', 'hx')
- velocity: float32 [4, 3, 16384], P('nb', None, 'hx')
The draws below stay inside these ranges and needn't reach their ends.
Inputs may be any that keep to these rules, and one draw needn't show every extreme that they name: `shared_slots`: rows j * 64 to (j + 1) * 64 - 1 of each device's 512 rows belong to owner j along hx. Each such block names exactly 16 distinct octants, each at least once; its other rows name one of these or are -1.
All inputs are finite; a program needn't handle non-finite values.
Results may differ from the reference program's by a relative error of at most 0.0048.
Values may be sent and summed in bfloat16 or wider, within the bound.
No kernel may reach another device: no remote copies, remote signals or barrier semaphores. Data moves between devices by JAX's collectives and lax.ppermute only.
A program may use at most 64 MiB of HBM per device.

```python
import math
import jax
import jax.numpy as jnp
from jax import lax

K = 1464
NT = 2
OCT_DEV = 1024
ROWS_DEV = 512
LEAVES = 16
PTS = 128
NBR = 8
CAP = 64
UNIQ = 16
OCTANTS = 8192
ROWS = 4096
LEAF_ALL = 128
POINTS = 16384
N_HX = 8
N_NB = 4


def draw_shared_slots(key, part):
    slot_total = N_NB * N_HX * N_HX
    subkeys = jax.random.split(key, 4)
    chosen = jax.vmap(lambda subkey: jax.random.permutation(subkey, OCT_DEV)[:UNIQ])(jax.random.split(subkeys[0], slot_total))
    live_count = jax.random.randint(subkeys[1], (slot_total,), UNIQ, CAP + 1)
    position = jnp.arange(CAP, dtype=jnp.int32)[None, :]
    picks = jax.random.randint(subkeys[2], (slot_total, CAP), 0, UNIQ)
    picks = jnp.where(position < UNIQ, jnp.minimum(position, UNIQ - 1), picks)
    slot_ids = jnp.take_along_axis(chosen, picks, axis=1)
    slot_ids = jnp.where(position < live_count[:, None], slot_ids, -1)
    shuffle = jax.vmap(lambda subkey: jax.random.permutation(subkey, CAP))(jax.random.split(subkeys[3], slot_total))
    slot_ids = jnp.take_along_axis(slot_ids, shuffle, axis=1)
    return slot_ids.reshape(N_NB, N_HX * N_HX * CAP).astype(jnp.int32)


def place_ends(values, key, least, high):
    index_at = [jax.random.randint(jax.random.fold_in(key, axis), (), 0, length) for axis, length in enumerate(values.shape)]
    widest = values.shape.index(max(values.shape))
    next_to = index_at[:widest] + [(index_at[widest] + 1) % values.shape[widest]] + index_at[widest + 1:]
    return values.at[tuple(index_at)].set(least).at[tuple(next_to)].set(high)


def steps_of(own_key, dims, pieces, least, high):
    loudness, own = 1.0, jax.random.fold_in(own_key, 6)
    for axis_at, blocks in pieces:
        draws = jnp.exp(jax.random.uniform(jax.random.fold_in(own, axis_at), (blocks,), jnp.float32, least / len(pieces), high / len(pieces)))
        loudness = loudness * jnp.repeat(draws, dims[axis_at] // blocks).reshape([-1 if axis == axis_at else 1 for axis in range(len(dims))])
    return loudness


def bell_draw(own_key, dims, scale, limit, cuts=(), kind=jnp.bfloat16):
    loudness = steps_of(own_key, dims, cuts, -0.22, 0.18) if cuts else 1.0
    values = jax.random.normal(own_key, dims, jnp.float32) * scale * loudness
    return jnp.minimum(jnp.maximum(values, -limit), limit).astype(kind)


def setup_inputs(seed: int = 0) -> dict:
    arg_keys = jax.random.split(jax.random.key(seed), 9)
    return {
        "partial_multipoles": bell_draw(arg_keys[0], (N_NB, ROWS, K), 1.0, 6.0, ((0, 4), (1, 8))),
        "shared_slots": draw_shared_slots(jax.random.fold_in(arg_keys[8], 71), 0),
        "m2l_sources": place_ends(jax.random.randint(arg_keys[2], (N_NB, NT, OCTANTS), 0, OCT_DEV), jax.random.fold_in(arg_keys[2], 1), 0, OCT_DEV - 1).astype(jnp.int32),
        "m2l_ops": bell_draw(arg_keys[3], (NT, K, K), K ** -0.5, 0.15625),
        "positions": jnp.clip(jax.random.uniform(arg_keys[4], (N_NB, 3, POINTS), jnp.float32, -1.0, 1.0) * steps_of(arg_keys[4], (N_NB, 3, POINTS), ((0, 4), (2, 8)), -0.4, 0.0), -1.0, 1.0),
        "forces": bell_draw(arg_keys[5], (N_NB, 3, POINTS), 1.0, 6.0, ((0, 4), (2, 8)), jnp.float32),
        "leaf_counts": place_ends(jax.random.randint(arg_keys[6], (N_NB, LEAF_ALL), PTS // 4, PTS + 1), jax.random.fold_in(arg_keys[6], 1), PTS // 4, PTS).astype(jnp.int32),
        "neighbours": place_ends(jax.random.randint(arg_keys[7], (N_NB, NBR, LEAF_ALL), 0, 3 * LEAVES), jax.random.fold_in(arg_keys[7], 1), 0, (3 * LEAVES) - 1).astype(jnp.int32),
    }


reg_eps2 = 0.01
inv_eight_pi = 1.0 / (8.0 * math.pi)

def leaf_velocity(target_pos, target_live, source_pos, source_frc):
    offset = target_pos[:, None, :] - source_pos[:, :, None]
    dist_sq = lax.optimization_barrier(jnp.sum(offset * offset, axis=0)) + reg_eps2
    inverse_cube = 1.0 / (dist_sq * jnp.sqrt(dist_sq))
    projected = lax.optimization_barrier(jnp.sum(source_frc[:, :, None] * offset, axis=0))
    summand = (source_frc[:, :, None] * (dist_sq + reg_eps2)[None] + projected[None] * offset) * inverse_cube[None]
    return lax.optimization_barrier(jnp.sum(summand, axis=1)) * inv_eight_pi * target_live[None, :]

def leaves_block(own_pos, own_live, leaf_lists, source_table):

    def one_leaf(item):
        leaf_pos, leaf_live, leaf_list = item
        chosen = source_table[:, leaf_list, :].reshape(6, -1)
        return leaf_velocity(leaf_pos, leaf_live, chosen[:3], chosen[3:])
    result = lax.map(one_leaf, (own_pos.transpose(1, 0, 2), own_live, leaf_lists.T))
    return result.transpose(1, 0, 2)

def far_field(partial_multipoles, shared_slots, m2l_sources, m2l_ops):
    row_count = partial_multipoles.shape[1]
    octants = m2l_sources.shape[2]
    owner = jnp.arange(row_count, dtype=jnp.int32) % ROWS_DEV // CAP
    block_base = jnp.arange(octants, dtype=jnp.int32) // OCT_DEV * OCT_DEV

    def one_slab(index):
        slot_ids = shared_slots[index]
        shard_rows = partial_multipoles[index]
        target = jnp.where(slot_ids >= 0, owner * OCT_DEV + slot_ids, octants).astype(jnp.int32)
        sums = jax.ops.segment_sum(shard_rows.astype(jnp.float32), target, num_segments=octants + 1)[:octants]
        multipoles = sums.astype(jnp.bfloat16)
        total = jnp.zeros((octants, multipoles.shape[1]), jnp.float32)
        for direction in range(NT):
            picked = multipoles[block_base + m2l_sources[index, direction]]
            total = total + jnp.dot(picked, m2l_ops[direction], preferred_element_type=jnp.float32)
        return total.astype(jnp.bfloat16)
    return lax.map(one_slab, jnp.arange(N_NB, dtype=jnp.int32))

def near_field(positions, forces, leaf_counts, neighbours):
    leaf_all = leaf_counts.shape[1]
    per_leaf = positions.shape[2] // leaf_all
    live = (jnp.arange(per_leaf, dtype=jnp.int32)[None, None, :] < leaf_counts[:, :, None]).astype(jnp.float32)
    pos_four = positions.reshape(N_NB, 3, leaf_all, per_leaf)
    frc_four = forces.reshape(N_NB, 3, leaf_all, per_leaf) * live[:, None]
    packed = jnp.concatenate([pos_four, frc_four], axis=1)
    padded = jnp.pad(packed, ((1, 1), (0, 0), (0, 0), (0, 0)))

    def one_block(index):
        zero = jnp.zeros((), jnp.int32)
        slab = (index // N_HX).astype(jnp.int32)
        member = (index % N_HX).astype(jnp.int32)
        start = (member * LEAVES).astype(jnp.int32)
        window = lax.dynamic_slice(padded, (slab, zero, start, zero), (3, 6, LEAVES, per_leaf))
        source_table = window.transpose(1, 0, 2, 3).reshape(6, 3 * LEAVES, per_leaf)
        own_pos = lax.dynamic_slice(pos_four, (slab, zero, start, zero), (1, 3, LEAVES, per_leaf))[0]
        own_live = lax.dynamic_slice(live, (slab, start, zero), (1, LEAVES, per_leaf))[0]
        leaf_lists = lax.dynamic_slice(neighbours, (slab, zero, start), (1, NBR, LEAVES))[0]
        return leaves_block(own_pos, own_live, leaf_lists, source_table)
    result = lax.map(one_block, jnp.arange(N_NB * N_HX, dtype=jnp.int32))
    result = result.reshape(N_NB, N_HX, 3, LEAVES, per_leaf).transpose(0, 2, 1, 3, 4)
    return result.reshape(N_NB, 3, leaf_all * per_leaf)

def reference(partial_multipoles, shared_slots, m2l_sources, m2l_ops, positions, forces, leaf_counts, neighbours):
    local_expansion = far_field(partial_multipoles, shared_slots, m2l_sources, m2l_ops)
    velocity = near_field(positions, forces, leaf_counts, neighbours)
    return (local_expansion, velocity)
```

```python
import functools
import math

import jax
import jax.numpy as jnp
from jax import lax
from jax.experimental import pallas as pl
from jax.experimental.pallas import tpu as pltpu
from jax.sharding import PartitionSpec as P

reg_eps2 = 0.01
inv_eight_pi = 1.0 / (8.0 * math.pi)
id_base = 32
lanes = 128
bf16 = jnp.bfloat16
f32 = jnp.float32


def split(value, count):
    pieces = []
    for _ in range(count):
        piece = value.astype(bf16).astype(f32)
        pieces.append(piece)
        value = value - piece
    return pieces


def presum_kernel(
    cap, uniq, counts_hbm, slots_hbm, rows_hbm, pos_hbm, frc_hbm, neighbours_hbm,
    sums_ref, packed_ref, counts_out, neighbours_out,
    counts_ref, slots_ref, rows_ref, pos_ref, frc_ref, arrival,
):
    pairs = (
        (slots_hbm, slots_ref),
        (counts_hbm, counts_ref),
        (pos_hbm, pos_ref),
        (frc_hbm, frc_ref),
        (counts_hbm, counts_out),
        (neighbours_hbm, neighbours_out),
        (rows_hbm, rows_ref),
    )
    copies = [pltpu.make_async_copy(a, b, arrival.at[i]) for i, (a, b) in enumerate(pairs)]
    for copy in copies:
        copy.start()
    for copy in copies[:-1]:
        copy.wait()

    leaves, per_leaf = pos_ref.shape[1:]
    leaf_at = lax.broadcasted_iota(jnp.int32, (leaves, per_leaf), 0)
    point_at = lax.broadcasted_iota(jnp.int32, (leaves, per_leaf), 1)
    count = jnp.zeros((leaves, per_leaf), jnp.int32)
    for leaf in range(leaves):
        count = jnp.where(leaf_at == leaf, counts_ref[0, leaf], count)
    live = (point_at < count).astype(f32)
    for axis in range(3):
        packed_ref[axis] = pos_ref[axis]
        packed_ref[3 + axis] = frc_ref[axis] * live

    coeffs, row_count = rows_ref.shape
    slot_count = sums_ref.shape[0]
    targets, firsts = [], []
    sub_at = lax.broadcasted_iota(jnp.int32, (lanes, lanes), 0)
    lane_at = lax.broadcasted_iota(jnp.int32, (lanes, lanes), 1)
    same_block = (sub_at // cap) == (lane_at // cap)
    for start in range(0, row_count, lanes):
        by_lane = jnp.broadcast_to(slots_ref[:, start : start + lanes], (lanes, lanes))
        by_sub = by_lane.T
        equal = same_block & (by_lane == by_sub)
        seen = jnp.where(equal & (lane_at < sub_at), 1, 0)
        first = (jnp.max(seen, axis=1, keepdims=True) == 0) & (by_sub >= 0)
        below = jnp.where(first & same_block & (by_sub < by_lane), 1, 0)
        rank = jnp.sum(below, axis=0, keepdims=True)
        lane_row = lax.broadcasted_iota(jnp.int32, (1, lanes), 1) + start
        block = lane_row // cap
        valid = slots_ref[:, start : start + lanes] >= 0
        targets.append(jnp.where(valid, block * uniq + rank, -1))
    target = jnp.concatenate(targets, axis=1)
    slot_at = lax.broadcasted_iota(jnp.int32, (slot_count, row_count), 0)
    hit = slot_at == target
    octant = jnp.max(jnp.where(hit, slots_ref[...], -1), axis=1, keepdims=True)
    one_hot = jnp.where(hit, 1.0, 0.0).astype(bf16)
    copies[-1].wait()
    sums = lax.dot_general(
        one_hot, rows_ref[...], (((1,), (1,)), ((), ())), preferred_element_type=f32
    )
    sums_ref[:, :coeffs] = sums.astype(bf16)
    high = octant // id_base
    low = octant - high * id_base
    extra_at = lax.broadcasted_iota(jnp.int32, (slot_count, sums_ref.shape[1] - coeffs), 1)
    extra = jnp.where(extra_at == 0, high, jnp.where(extra_at == 1, low, 0))
    sums_ref[:, coeffs:] = extra.astype(f32).astype(bf16)


def near_kernel(
    slab_axis, neighbours_ref, counts_ref, own_ref, even_ref, odd_ref, out_ref,
    wide_ref, source_ref, target_wide_ref, target_ref,
):
    _, leaves, per_leaf = own_ref.shape
    group = 8
    wide = 3 * group
    deep = 4 * group
    nbr_count = neighbours_ref.shape[1]
    even = lax.rem(lax.axis_index(slab_axis), 2) == 0

    def stored(ref, leaf_start, height, row, value):
        ref[pl.ds(leaf_start * height + row, leaves, stride=height), :] = value

    for part in range(3):
        if part == 0:
            comp = [jnp.where(even, odd_ref[c], even_ref[c]) for c in range(6)]
        elif part == 1:
            comp = [own_ref[c] for c in range(6)]
        else:
            comp = [jnp.where(even, even_ref[c], odd_ref[c]) for c in range(6)]
        cut = [split(c, 2) for c in comp]
        kept = [high + low for high, low in cut]
        norm = kept[0] * kept[0] + kept[1] * kept[1] + kept[2] * kept[2]
        size = split(norm + reg_eps2, 3)
        along = split(-(kept[0] * kept[3] + kept[1] * kept[4] + kept[2] * kept[5]), 3)
        for piece in range(2):
            rows = [cut[c][piece] for c in range(6)] + [size[piece], along[piece]]
            for row, value in enumerate(rows):
                stored(wide_ref, part * leaves, wide, piece * group + row, value)
        stored(wide_ref, part * leaves, wide, 2 * group, size[2])
        stored(wide_ref, part * leaves, wide, 2 * group + 1, along[2])
        if part == 1:
            norm = split(norm, 3)
            zero, one = jnp.zeros_like(norm[0]), jnp.ones_like(norm[0])
            for piece in range(2):
                fill = [one, one] if piece == 0 else [zero, zero]
                rows = [-2.0 * cut[c][piece] for c in range(3)] + [cut[c][piece] for c in range(3)] + fill
                for row, value in enumerate(rows):
                    stored(target_wide_ref, 0, 2 * wide, piece * 2 * group + row, value)
                    stored(target_wide_ref, 0, 2 * wide, piece * 2 * group + group + row, value)
            for row, value in enumerate([one, one] + norm + [zero] * (2 * group - 5)):
                stored(target_wide_ref, 0, 2 * wide, 4 * group + row, value)

    row_at = lax.broadcasted_iota(jnp.int32, (group, per_leaf), 0)
    left = (row_at < 3) | (row_at == 6)
    left_ones = (row_at >= 2) & (row_at < 5)
    for leaf in range(3 * leaves):
        high, low, rest = [wide_ref[pl.ds(leaf * wide + i * group, group), :] for i in range(3)]
        for half in range(2):
            if half == 0:
                tail = jnp.where(row_at == 0, rest, jnp.where(left_ones, 1.0, 0.0))
                pieces = [jnp.where(left, high, 0.0), jnp.where(left, low, 0.0), tail]
            else:
                tail = jnp.where(row_at == 1, rest, 0.0)
                pieces = [jnp.where(left, 0.0, high), jnp.where(left, 0.0, low), tail]
            pieces.append(jnp.zeros((group, per_leaf), f32))
            block = jnp.concatenate(pieces, axis=0).astype(bf16)
            source_ref[pl.ds(leaf * deep, deep), pl.ds(half * per_leaf, per_leaf)] = block
    for leaf in range(leaves):
        block = target_wide_ref[pl.ds(leaf * 2 * wide, 2 * wide), :]
        target_ref[pl.ds(leaf * per_leaf, per_leaf), :] = block.T.astype(bf16)

    def one_leaf(leaf, carry):
        target = target_ref[pl.ds(pl.multiple_of(leaf * per_leaf, per_leaf), per_leaf), :]
        total = jnp.zeros((per_leaf, deep), f32)
        for n in range(nbr_count):
            source = neighbours_ref[0, n, leaf]
            block = source_ref[pl.ds(pl.multiple_of(source * deep, deep), deep), :]
            features = jnp.concatenate([block[: 2 * group], block], axis=0)
            both = jnp.dot(target, features, preferred_element_type=f32)
            dist_sq, projected = both[:, :per_leaf], both[:, per_leaf:]
            inverse = lax.rsqrt(dist_sq)
            cube = inverse * inverse * inverse
            along_f = inverse + reg_eps2 * cube
            along_d = projected * cube
            pair = jnp.concatenate([along_d.astype(bf16), along_f.astype(bf16)], axis=1)
            total = total + lax.dot_general(
                pair, block, (((1,), (1,)), ((), ())), preferred_element_type=f32
            )
        turned = total.T
        live = lax.broadcasted_iota(jnp.int32, (1, per_leaf), 1) < counts_ref[0, leaf]
        factor = jnp.where(live, inv_eight_pi, 0.0)
        weight = turned[18:19]
        for axis in range(3):
            own = own_ref[axis, pl.ds(leaf, 1), :]
            along_f = turned[3 + axis : 4 + axis] + turned[11 + axis : 12 + axis]
            along_y = turned[axis : axis + 1] + turned[8 + axis : 9 + axis]
            out_ref[axis, pl.ds(leaf, 1), :] = (along_f + (own * weight - along_y)) * factor
        return carry

    lax.fori_loop(0, leaves, one_leaf, 0, unroll=8)


def far_kernel(sources_ref, rows_ref, ops_hbm, out_hbm, ops_ref, pick_ref, moved_ref, out_ref, ops_sem, out_sem):
    coeffs = ops_hbm.shape[1]
    directions = ops_hbm.shape[0]
    slot_count = rows_ref.shape[0]
    tile = moved_ref.shape[1]
    spans = [(start, min(tile, coeffs - start)) for start in range(0, coeffs, tile)]

    loads = []
    for i, (start, size) in enumerate(spans):
        at = pl.ds(start, size)
        loads.append(pltpu.make_async_copy(ops_hbm.at[:, :, at], ops_ref.at[:, :, at], ops_sem.at[i]))
        loads[-1].start()

    octant = rows_ref[:, coeffs : coeffs + 2].astype(f32).astype(jnp.int32)
    octant = octant[:, :1] * id_base + octant[:, 1:]
    for t in range(directions):
        hit = octant == sources_ref[0, t : t + 1, :]
        pick_ref[t * slot_count : (t + 1) * slot_count, :] = jnp.where(hit, 1.0, 0.0).astype(bf16)
    rows = rows_ref[:, :coeffs]
    stores = []
    for i, (start, size) in enumerate(spans):
        loads[i].wait()
        for t in range(directions):
            moved = jnp.dot(rows, ops_ref[t, :, start : start + size], preferred_element_type=f32)
            moved_ref[t * slot_count : (t + 1) * slot_count, :size] = moved.astype(bf16)
        total = lax.dot_general(
            moved_ref[:, :size], pick_ref[...], (((0,), (0,)), ((), ())), preferred_element_type=f32
        )
        out_ref[start : start + size, :] = total.astype(bf16)
        at = pl.ds(start, size)
        stores.append(pltpu.make_async_copy(out_ref.at[at, :], out_hbm.at[at, :], out_sem.at[i]))
        stores[-1].start()
    for store in stores:
        store.wait()


def vmem():
    return pl.BlockSpec(memory_space=pltpu.VMEM)


def in_hbm(array):
    return pltpu.with_memory_space_constraint(array, pltpu.HBM)


def smem():
    return pl.BlockSpec(memory_space=pltpu.SMEM)


def call_near(neighbours, leaf_counts, packed, even, odd):
    _, leaves, per_leaf = packed.shape
    table = 3 * leaves
    return pl.pallas_call(
        functools.partial(near_kernel, "nb"),
        out_shape=jax.ShapeDtypeStruct((3, leaves, per_leaf), f32),
        in_specs=[smem(), smem()] + [vmem()] * 3,
        out_specs=vmem(),
        scratch_shapes=[
            pltpu.VMEM((table * 24, per_leaf), f32),
            pltpu.VMEM((table * 32, 2 * per_leaf), bf16),
            pltpu.VMEM((leaves * 48, per_leaf), f32),
            pltpu.VMEM((leaves * per_leaf, 48), bf16),
        ],
        compiler_params=pltpu.CompilerParams(vmem_limit_bytes=24 * 2**20),
        cost_estimate=pl.CostEstimate(flops=8 * 10**9, bytes_accessed=10**6, transcendentals=2 * 10**6),
        name="near",
    )(neighbours, leaf_counts, packed, even, odd)


def on_device(
    partial_multipoles,
    shared_slots,
    m2l_sources,
    m2l_ops,
    positions,
    forces,
    leaf_counts,
    neighbours,
):
    hx_count, nb_count = lax.axis_size("hx"), lax.axis_size("nb")
    row_count, coeffs = partial_multipoles.shape[1:]
    cap = row_count // hx_count
    uniq = cap // 4
    slot_count = hx_count * uniq
    width = -(-(coeffs + 2) // lanes) * lanes
    leaves = leaf_counts.shape[1]
    per_leaf = positions.shape[2] // leaves
    owned = m2l_sources.shape[2]
    directions = m2l_ops.shape[0]

    sums, packed, counts, sources = pl.pallas_call(
        functools.partial(presum_kernel, cap, uniq),
        out_shape=(
            pltpu.VMEM((slot_count, width), bf16),
            pltpu.VMEM((6, leaves, per_leaf), f32),
            pltpu.VMEM(leaf_counts.shape, jnp.int32),
            pltpu.VMEM(neighbours.shape, jnp.int32),
        ),
        in_specs=[pl.BlockSpec(memory_space=pltpu.HBM)] * 6,
        out_specs=(vmem(), vmem(), vmem(), vmem()),
        scratch_shapes=[
            pltpu.SMEM(leaf_counts.shape, jnp.int32),
            pltpu.VMEM(shared_slots.shape, jnp.int32),
            pltpu.VMEM((coeffs, row_count), bf16),
            pltpu.VMEM((3, leaves, per_leaf), f32),
            pltpu.VMEM((3, leaves, per_leaf), f32),
            pltpu.SemaphoreType.DMA((7,)),
        ],
        compiler_params=pltpu.CompilerParams(vmem_limit_bytes=16 * 2**20),
        name="presum",
    )(
        *map(
            in_hbm,
            (
                leaf_counts,
                shared_slots,
                partial_multipoles[0].T,
                positions[0].reshape(3, leaves, per_leaf),
                forces[0].reshape(3, leaves, per_leaf),
                neighbours,
            ),
        )
    )

    even_pairs = [(i, i + 1) for i in range(0, nb_count - 1, 2)]
    odd_pairs = [(i, i + 1) for i in range(1, nb_count - 1, 2)]
    odd = lax.ppermute(packed, "nb", odd_pairs + [(j, i) for i, j in odd_pairs])
    even = lax.ppermute(packed, "nb", even_pairs + [(j, i) for i, j in even_pairs])
    arrived = lax.all_to_all(
        sums.reshape(hx_count, uniq, width), "hx", split_axis=0, concat_axis=0, tiled=True
    ).reshape(slot_count, width)

    velocity = call_near(sources, counts, packed, even, odd)

    tile = 2 * lanes
    steps = -(-coeffs // tile)
    local = pl.pallas_call(
        far_kernel,
        out_shape=jax.ShapeDtypeStruct((coeffs, owned), bf16),
        in_specs=[vmem(), vmem(), pl.BlockSpec(memory_space=pltpu.HBM)],
        out_specs=pl.BlockSpec(memory_space=pltpu.HBM),
        scratch_shapes=[
            pltpu.VMEM(m2l_ops.shape, bf16),
            pltpu.VMEM((directions * slot_count, owned), bf16),
            pltpu.VMEM((directions * slot_count, tile), bf16),
            pltpu.VMEM((coeffs, owned), bf16),
            pltpu.SemaphoreType.DMA((steps,)),
            pltpu.SemaphoreType.DMA((steps,)),
        ],
        compiler_params=pltpu.CompilerParams(vmem_limit_bytes=32 * 2**20),
        name="far",
    )(m2l_sources, arrived, in_hbm(m2l_ops))

    return local.T[None], velocity.reshape(1, 3, leaves * per_leaf)


def solution(mesh):
    placed = (
        P("nb", "hx", None),
        P("nb", "hx"),
        P("nb", None, "hx"),
        P(),
        P("nb", None, "hx"),
        P("nb", None, "hx"),
        P("nb", "hx"),
        P("nb", None, "hx"),
    )
    return jax.shard_map(
        on_device,
        mesh=mesh,
        in_specs=placed,
        out_specs=(P("nb", "hx", None), P("nb", None, "hx")),
        check_vma=False,
    )
```

```python
import functools
import math

import jax
import jax.numpy as jnp
from jax import lax
from jax.experimental import pallas as pl
from jax.experimental.pallas import tpu as pltpu
from jax.sharding import PartitionSpec as P

reg_eps2 = 0.01
inv_eight_pi = 1.0 / (8.0 * math.pi)
id_base = 32
lanes = 128
bf16 = jnp.bfloat16
f32 = jnp.float32


def split(value, count):
    pieces = []
    for _ in range(count):
        piece = value.astype(bf16).astype(f32)
        pieces.append(piece)
        value = value - piece
    return pieces


def presum_kernel(
    cap, uniq, tile, counts_hbm, slots_hbm, rows_hbm, pos_hbm, frc_hbm, neighbours_hbm,
    sums_hbm, packed_ref, counts_out, neighbours_out,
    counts_ref, slots_ref, rows_ref, pos_ref, frc_ref, sums_ref, arrival, rows_sem, sums_sem,
):
    coeffs, row_count = rows_ref.shape
    slot_count, width = sums_ref.shape
    spans = [(start, min(tile, coeffs - start)) for start in range(0, coeffs, tile)]
    pairs = (
        (slots_hbm, slots_ref),
        (counts_hbm, counts_ref),
        (pos_hbm, pos_ref),
        (frc_hbm, frc_ref),
        (counts_hbm, counts_out),
        (neighbours_hbm, neighbours_out),
    )
    copies = [pltpu.make_async_copy(a, b, arrival.at[i]) for i, (a, b) in enumerate(pairs)]
    loads = []
    for i, (start, size) in enumerate(spans):
        at = pl.ds(start, size)
        loads.append(pltpu.make_async_copy(rows_hbm.at[at, :], rows_ref.at[at, :], rows_sem.at[i]))
    for copy in copies[:1] + loads + copies[1:]:
        copy.start()
    copies[0].wait()

    targets = []
    sub_at = lax.broadcasted_iota(jnp.int32, (lanes, lanes), 0)
    lane_at = lax.broadcasted_iota(jnp.int32, (lanes, lanes), 1)
    same_block = (sub_at // cap) == (lane_at // cap)
    for start in range(0, row_count, lanes):
        by_lane = jnp.broadcast_to(slots_ref[:, start : start + lanes], (lanes, lanes))
        by_sub = by_lane.T
        equal = same_block & (by_lane == by_sub)
        seen = jnp.where(equal & (lane_at < sub_at), 1, 0)
        first = (jnp.max(seen, axis=1, keepdims=True) == 0) & (by_sub >= 0)
        below = jnp.where(first & same_block & (by_sub < by_lane), 1, 0)
        rank = jnp.sum(below, axis=0, keepdims=True)
        lane_row = lax.broadcasted_iota(jnp.int32, (1, lanes), 1) + start
        block = lane_row // cap
        valid = slots_ref[:, start : start + lanes] >= 0
        targets.append(jnp.where(valid, block * uniq + rank, -1))
    target = jnp.concatenate(targets, axis=1)
    slot_at = lax.broadcasted_iota(jnp.int32, (slot_count, row_count), 0)
    hit = slot_at == target
    octant = jnp.max(jnp.where(hit, slots_ref[...], -1), axis=1, keepdims=True)
    one_hot = jnp.where(hit, 1.0, 0.0).astype(bf16)
    high = octant // id_base
    low = octant - high * id_base
    extra_at = lax.broadcasted_iota(jnp.int32, (slot_count, width - coeffs), 1)
    extra = jnp.where(extra_at == 0, high, jnp.where(extra_at == 1, low, 0))
    sums_ref[:, coeffs:] = extra.astype(f32).astype(bf16)
    stores = []
    for i, (start, size) in enumerate(spans):
        loads[i].wait()
        sums = lax.dot_general(
            one_hot,
            rows_ref[start : start + size, :],
            (((1,), (1,)), ((), ())),
            preferred_element_type=f32,
        )
        sums_ref[:, start : start + size] = sums.astype(bf16)
        at = pl.ds(start, min(tile, width - start))
        stores.append(pltpu.make_async_copy(sums_ref.at[:, at], sums_hbm.at[:, at], sums_sem.at[i]))
        stores[-1].start()
    for copy in copies[1:]:
        copy.wait()
    leaves, per_leaf = pos_ref.shape[1:]
    leaf_at = lax.broadcasted_iota(jnp.int32, (leaves, per_leaf), 0)
    point_at = lax.broadcasted_iota(jnp.int32, (leaves, per_leaf), 1)
    count = jnp.zeros((leaves, per_leaf), jnp.int32)
    for leaf in range(leaves):
        count = jnp.where(leaf_at == leaf, counts_ref[0, leaf], count)
    live = (point_at < count).astype(f32)
    for axis in range(3):
        packed_ref[axis] = pos_ref[axis]
        packed_ref[3 + axis] = frc_ref[axis] * live
    for store in stores:
        store.wait()


def near_field(
    slab_axis, lists, neighbours_ref, counts_ref, own_ref, even_ref, odd_ref, out_ref,
    point_ref, moment_ref, source_ref, weight_ref, target_wide_ref, target_ref, sums_ref,
):
    _, leaves, per_leaf = own_ref.shape
    group = 16
    pieces = 3
    nbr_count = neighbours_ref.shape[1]
    even = lax.rem(lax.axis_index(slab_axis), 2) == 0
    one = jnp.ones((leaves, per_leaf), f32)

    def stored(ref, leaf_start, height, rows):
        for row, value in enumerate(rows):
            ref[pl.ds(leaf_start * height + row, leaves, stride=height), :] = value

    def dot3(left, right):
        return left[0] * right[0] + left[1] * right[1] + left[2] * right[2]

    own_cut = None
    for part in range(3):
        if part == 0:
            comp = [jnp.where(even, odd_ref[c], even_ref[c]) for c in range(6)]
        elif part == 1:
            comp = [own_ref[c] for c in range(6)]
        else:
            comp = [jnp.where(even, even_ref[c], odd_ref[c]) for c in range(6)]
        cut = [split(c, 2) for c in comp[:3]]
        place = [high + low for high, low in cut]
        force = comp[3:]
        norm = dot3(place, place)
        along = dot3(force, place)
        size = split(norm + reg_eps2, 3)
        stored(point_ref, part * leaves, group, [c[0] for c in cut] + [c[1] for c in cut] + size)
        moments = force + [force[i] * place[j] for i in range(3) for j in range(3)]
        moments += [force[i] * (norm + 2.0 * reg_eps2) + along * place[i] for i in range(3)]
        stored(moment_ref, part * leaves, group, moments)
        if part == 1:
            own_cut, own_norm, own_place = cut, norm, place
    high = [-2.0 * c[0] for c in own_cut]
    low = [-2.0 * c[1] for c in own_cut]
    zero = jnp.zeros_like(one)
    rows = high + high + [one] * 3 + split(own_norm, 3) + [zero] * 4 + low + low + [zero] * 10
    stored(target_wide_ref, 0, 2 * group, rows)

    row_at = lax.broadcasted_iota(jnp.int32, (group, per_leaf), 0)
    for leaf in range(3 * leaves):
        at = pl.ds(leaf * group, group)
        point = jnp.where(row_at < 9, point_ref[at, :], jnp.where(row_at < 12, 1.0, 0.0))
        source_ref[at, :] = point.astype(bf16)
        moment = jnp.where(row_at < 15, moment_ref[at, :], 0.0)
        for i, piece in enumerate(split(moment, pieces)):
            weight_ref[pl.ds((leaf * pieces + i) * group, group), :] = piece.astype(bf16)
    for leaf in range(leaves):
        block = target_wide_ref[pl.ds(leaf * 2 * group, 2 * group), :]
        target_ref[pl.ds(leaf * per_leaf, per_leaf), :] = block.T.astype(bf16)

    for copy in lists:
        copy.wait()

    def one_leaf(leaf, carry):
        target = target_ref[pl.ds(pl.multiple_of(leaf * per_leaf, per_leaf), per_leaf), :]
        total = jnp.zeros((per_leaf, pieces * group), f32)
        for n in range(0, nbr_count, 2):
            near = [neighbours_ref[0, n + k, leaf] for k in range(2)]
            points = [source_ref[pl.ds(pl.multiple_of(s * group, group), group), :] for s in near]
            deep = pieces * group
            weights = [weight_ref[pl.ds(pl.multiple_of(s * deep, group), deep), :] for s in near]
            points = jnp.concatenate(points, axis=1)
            dist_sq = jnp.dot(
                target, jnp.concatenate([points, points], axis=0), preferred_element_type=f32
            )
            inverse = lax.rsqrt(dist_sq)
            cube = (inverse * inverse * inverse).astype(bf16)
            total = total + lax.dot_general(
                cube,
                jnp.concatenate(weights, axis=1),
                (((1,), (1,)), ((), ())),
                preferred_element_type=f32,
            )
        turned = total.T
        sums = turned[:group] + turned[group : 2 * group] + turned[2 * group :]
        sums_ref[pl.ds(leaf, group, stride=leaves), :] = sums
        return carry

    lax.fori_loop(0, leaves, one_leaf, 0, unroll=8)

    got = [sums_ref[pl.ds(row * leaves, leaves), :] for row in range(15)]
    first, mixed, rest = got[:3], [got[3 + 3 * i : 6 + 3 * i] for i in range(3)], got[12:]
    leaf_at = lax.broadcasted_iota(jnp.int32, (leaves, per_leaf), 0)
    point_at = lax.broadcasted_iota(jnp.int32, (leaves, per_leaf), 1)
    count = jnp.zeros((leaves, per_leaf), jnp.int32)
    for leaf in range(leaves):
        count = jnp.where(leaf_at == leaf, counts_ref[0, leaf], count)
    factor = jnp.where(point_at < count, inv_eight_pi, 0.0)
    shift = dot3(own_place, first) - (mixed[0][0] + mixed[1][1] + mixed[2][2])
    for i in range(3):
        turned = dot3(own_place, [2.0 * mixed[i][j] + mixed[j][i] for j in range(3)])
        out_ref[i] = (own_norm * first[i] + own_place[i] * shift - turned + rest[i]) * factor


def far_field(sources_ref, rows_ref, ops_ref, out_ref, out_hbm, pick_ref, moved_ref, out_sem, ready):
    directions, coeffs, _ = ops_ref.shape
    slot_count = rows_ref.shape[0]
    tile = moved_ref.shape[1]
    octant = rows_ref[:, coeffs : coeffs + 2].astype(f32).astype(jnp.int32)
    octant = octant[:, :1] * id_base + octant[:, 1:]
    for t in range(directions):
        hit = octant == sources_ref[0, t : t + 1, :]
        pick_ref[t * slot_count : (t + 1) * slot_count, :] = jnp.where(hit, 1.0, 0.0).astype(bf16)
    rows = rows_ref[:, :coeffs]
    stores = []
    for i, start in enumerate(range(0, coeffs, tile)):
        ready(i)
        size = min(tile, coeffs - start)
        for t in range(directions):
            moved = jnp.dot(rows, ops_ref[t, :, start : start + size], preferred_element_type=f32)
            moved_ref[t * slot_count : (t + 1) * slot_count, :size] = moved.astype(bf16)
        for low in range(0, size, 2 * lanes):
            rest = min(2 * lanes, size - low)
            total = lax.dot_general(
                moved_ref[:, low : low + rest],
                pick_ref[...],
                (((0,), (0,)), ((), ())),
                preferred_element_type=f32,
            )
            at = pl.ds(start + low, rest)
            out_ref[at, :] = total.astype(bf16)
            sem = out_sem.at[len(stores)]
            stores.append(pltpu.make_async_copy(out_ref.at[at, :], out_hbm.at[at, :], sem))
            stores[-1].start()
    return stores


def fields_kernel(
    slab_axis, neighbours_vmem, counts_vmem, own_ref, odd_ref, even_ref, picks_hbm, rows_ref, ops_hbm,
    velocity_hbm, local_hbm,
    neighbours_ref, counts_ref, velocity_ref,
    point_ref, moment_ref, source_ref, weight_ref, target_wide_ref, target_ref, sums_ref,
    picks_ref, ops_ref, pick_ref, moved_ref, local_ref, ops_sem, out_sem,
):
    coeffs, tile = ops_hbm.shape[1], moved_ref.shape[1]
    steps = -(-coeffs // tile)
    lists = (
        pltpu.make_async_copy(neighbours_vmem, neighbours_ref, ops_sem.at[steps + 1]),
        pltpu.make_async_copy(counts_vmem, counts_ref, ops_sem.at[steps + 2]),
    )
    for copy in lists:
        copy.start()
    picks_load = pltpu.make_async_copy(picks_hbm, picks_ref, ops_sem.at[steps])
    picks_load.start()
    loads = []
    for i, start in enumerate(range(0, coeffs, tile)):
        at = pl.ds(start, min(tile, coeffs - start))
        loads.append(pltpu.make_async_copy(ops_hbm.at[:, :, at], ops_ref.at[:, :, at], ops_sem.at[i]))
        loads[-1].start()
    near_field(
        slab_axis, lists, neighbours_ref, counts_ref, own_ref, even_ref, odd_ref, velocity_ref,
        point_ref, moment_ref, source_ref, weight_ref, target_wide_ref, target_ref, sums_ref,
    )
    velocity_store = pltpu.make_async_copy(velocity_ref, velocity_hbm, ops_sem.at[steps + 3])
    velocity_store.start()
    picks_load.wait()
    stores = far_field(
        picks_ref, rows_ref, ops_ref, local_ref, local_hbm, pick_ref, moved_ref, out_sem,
        lambda i: loads[i].wait(),
    )
    for store in stores + [velocity_store]:
        store.wait()


def vmem():
    return pl.BlockSpec(memory_space=pltpu.VMEM)


def in_hbm(array):
    return pltpu.with_memory_space_constraint(array, pltpu.HBM)


def hbm():
    return pl.BlockSpec(memory_space=pltpu.HBM)


def call_fields(neighbours, leaf_counts, packed, even, odd, m2l_sources, arrived, m2l_ops):
    _, leaves, per_leaf = packed.shape
    directions, coeffs, _ = m2l_ops.shape
    owned = m2l_sources.shape[2]
    slot_count = arrived.shape[0]
    tile = 4 * lanes
    steps = -(-coeffs // tile)
    table = 3 * leaves
    picks = directions * slot_count
    return pl.pallas_call(
        functools.partial(fields_kernel, "nb"),
        out_shape=(
            jax.ShapeDtypeStruct((3, leaves, per_leaf), f32),
            jax.ShapeDtypeStruct((coeffs, owned), bf16),
        ),
        in_specs=[vmem(), vmem(), vmem(), vmem(), vmem(), hbm(), vmem(), hbm()],
        out_specs=(hbm(), hbm()),
        scratch_shapes=[
            pltpu.SMEM(neighbours.shape, jnp.int32),
            pltpu.SMEM(leaf_counts.shape, jnp.int32),
            pltpu.VMEM((3, leaves, per_leaf), f32),
            pltpu.VMEM((table * 16, per_leaf), f32),
            pltpu.VMEM((table * 16, per_leaf), f32),
            pltpu.VMEM((table * 16, per_leaf), bf16),
            pltpu.VMEM((table * 48, per_leaf), bf16),
            pltpu.VMEM((leaves * 32, per_leaf), f32),
            pltpu.VMEM((leaves * per_leaf, 32), bf16),
            pltpu.VMEM((16 * leaves, per_leaf), f32),
            pltpu.VMEM(m2l_sources.shape, jnp.int32),
            pltpu.VMEM(m2l_ops.shape, bf16),
            pltpu.VMEM((picks, owned), bf16),
            pltpu.VMEM((picks, tile), bf16),
            pltpu.VMEM((coeffs, owned), bf16),
            pltpu.SemaphoreType.DMA((steps + 4,)),
            pltpu.SemaphoreType.DMA((-(-coeffs // (2 * lanes)),)),
        ],
        compiler_params=pltpu.CompilerParams(vmem_limit_bytes=40 * 2**20),
        name="fields",
    )(neighbours, leaf_counts, packed, odd, even, in_hbm(m2l_sources), arrived, in_hbm(m2l_ops))


def call_presum(hx_count, partial_multipoles, shared_slots, positions, forces, leaf_counts, neighbours):
    row_count, coeffs = partial_multipoles.shape[1:]
    cap = row_count // hx_count
    uniq = cap // 4
    slot_count = hx_count * uniq
    width = -(-(coeffs + 2) // lanes) * lanes
    tile = width
    steps = -(-coeffs // tile)
    leaves = leaf_counts.shape[1]
    per_leaf = positions.shape[2] // leaves

    return pl.pallas_call(
        functools.partial(presum_kernel, cap, uniq, tile),
        out_shape=(
            jax.ShapeDtypeStruct((slot_count, width), bf16),
            pltpu.VMEM((6, leaves, per_leaf), f32),
            pltpu.VMEM(leaf_counts.shape, jnp.int32),
            pltpu.VMEM(neighbours.shape, jnp.int32),
        ),
        in_specs=[hbm()] * 6,
        out_specs=(hbm(), vmem(), vmem(), vmem()),
        scratch_shapes=[
            pltpu.SMEM(leaf_counts.shape, jnp.int32),
            pltpu.VMEM(shared_slots.shape, jnp.int32),
            pltpu.VMEM((coeffs, row_count), bf16),
            pltpu.VMEM((3, leaves, per_leaf), f32),
            pltpu.VMEM((3, leaves, per_leaf), f32),
            pltpu.VMEM((slot_count, width), bf16),
            pltpu.SemaphoreType.DMA((6,)),
            pltpu.SemaphoreType.DMA((steps,)),
            pltpu.SemaphoreType.DMA((steps,)),
        ],
        compiler_params=pltpu.CompilerParams(vmem_limit_bytes=16 * 2**20),
        name="presum",
    )(
        *map(
            in_hbm,
            (
                leaf_counts,
                shared_slots,
                partial_multipoles[0].T,
                positions[0].reshape(3, leaves, per_leaf),
                forces[0].reshape(3, leaves, per_leaf),
                neighbours,
            ),
        )
    )


def on_device(
    partial_multipoles,
    shared_slots,
    m2l_sources,
    m2l_ops,
    positions,
    forces,
    leaf_counts,
    neighbours,
):
    hx_count, nb_count = lax.axis_size("hx"), lax.axis_size("nb")
    sums, packed, counts, sources = call_presum(
        hx_count, partial_multipoles, shared_slots, positions, forces, leaf_counts, neighbours
    )

    even_pairs = [(i, i + 1) for i in range(0, nb_count - 1, 2)]
    odd_pairs = [(i, i + 1) for i in range(1, nb_count - 1, 2)]
    odd = lax.ppermute(packed, "nb", odd_pairs + [(j, i) for i, j in odd_pairs])
    even = lax.ppermute(packed, "nb", even_pairs + [(j, i) for i, j in even_pairs])
    arrived = lax.all_to_all(
        sums.reshape(hx_count, -1, sums.shape[1]), "hx", split_axis=0, concat_axis=0, tiled=True
    ).reshape(sums.shape)

    velocity, local = call_fields(sources, counts, packed, even, odd, m2l_sources, arrived, m2l_ops)

    return local.T[None], velocity.reshape(positions.shape)


def solution(mesh):
    placed = (
        P("nb", "hx", None),
        P("nb", "hx"),
        P("nb", None, "hx"),
        P(),
        P("nb", None, "hx"),
        P("nb", None, "hx"),
        P("nb", "hx"),
        P("nb", None, "hx"),
    )
    return jax.shard_map(
        on_device,
        mesh=mesh,
        in_specs=placed,
        out_specs=(P("nb", "hx", None), P("nb", None, "hx")),
        check_vma=False,
    )
```

```python
import functools
import math

import jax
import jax.numpy as jnp
from jax import lax
from jax.experimental import pallas as pl
from jax.experimental.pallas import tpu as pltpu
from jax.sharding import PartitionSpec as P

reg_eps2 = 0.01
inv_eight_pi = 1.0 / (8.0 * math.pi)
id_base = 32
lanes = 128
bf16 = jnp.bfloat16
f32 = jnp.float32


def split(value, count):
    pieces = []
    for _ in range(count):
        piece = value.astype(bf16).astype(f32)
        pieces.append(piece)
        value = value - piece
    return pieces


def presum_kernel(
    cap, uniq, tile, counts_hbm, slots_hbm, rows_hbm, pos_hbm, frc_hbm, neighbours_hbm,
    sums_hbm, packed_ref, live_ref, neighbours_out,
    counts_ref, slots_ref, rows_ref, pos_ref, frc_ref, sums_ref, arrival, rows_sem, sums_sem,
):
    coeffs, row_count = rows_ref.shape
    slot_count, width = sums_ref.shape
    spans = [(start, min(tile, coeffs - start)) for start in range(0, coeffs, tile)]
    pairs = (
        (slots_hbm, slots_ref),
        (counts_hbm, counts_ref),
        (pos_hbm, pos_ref),
        (frc_hbm, frc_ref),
        (neighbours_hbm, neighbours_out),
    )
    copies = [pltpu.make_async_copy(a, b, arrival.at[i]) for i, (a, b) in enumerate(pairs)]
    loads = []
    for i, (start, size) in enumerate(spans):
        at = pl.ds(start, size)
        loads.append(pltpu.make_async_copy(rows_hbm.at[at, :], rows_ref.at[at, :], rows_sem.at[i]))
    for copy in copies[:1] + loads + copies[1:]:
        copy.start()
    copies[0].wait()

    targets = []
    sub_at = lax.broadcasted_iota(jnp.int32, (lanes, lanes), 0)
    lane_at = lax.broadcasted_iota(jnp.int32, (lanes, lanes), 1)
    same_block = (sub_at // cap) == (lane_at // cap)
    for start in range(0, row_count, lanes):
        by_lane = jnp.broadcast_to(slots_ref[:, start : start + lanes], (lanes, lanes))
        by_sub = by_lane.T
        equal = same_block & (by_lane == by_sub)
        seen = jnp.where(equal & (lane_at < sub_at), 1, 0)
        first = (jnp.max(seen, axis=1, keepdims=True) == 0) & (by_sub >= 0)
        below = jnp.where(first & same_block & (by_sub < by_lane), 1, 0)
        rank = jnp.sum(below, axis=0, keepdims=True)
        lane_row = lax.broadcasted_iota(jnp.int32, (1, lanes), 1) + start
        block = lane_row // cap
        valid = slots_ref[:, start : start + lanes] >= 0
        targets.append(jnp.where(valid, block * uniq + rank, -1))
    target = jnp.concatenate(targets, axis=1)
    slot_at = lax.broadcasted_iota(jnp.int32, (slot_count, row_count), 0)
    hit = slot_at == target
    octant = jnp.max(jnp.where(hit, slots_ref[...], -1), axis=1, keepdims=True)
    one_hot = jnp.where(hit, 1.0, 0.0).astype(bf16)
    high = octant // id_base
    low = octant - high * id_base
    extra_at = lax.broadcasted_iota(jnp.int32, (slot_count, width - coeffs), 1)
    extra = jnp.where(extra_at == 0, high, jnp.where(extra_at == 1, low, 0))
    sums_ref[:, coeffs:] = extra.astype(f32).astype(bf16)
    stores = []
    for i, (start, size) in enumerate(spans):
        loads[i].wait()
        sums = lax.dot_general(
            one_hot,
            rows_ref[start : start + size, :],
            (((1,), (1,)), ((), ())),
            preferred_element_type=f32,
        )
        sums_ref[:, start : start + size] = sums.astype(bf16)
        at = pl.ds(start, min(tile, width - start))
        stores.append(pltpu.make_async_copy(sums_ref.at[:, at], sums_hbm.at[:, at], sums_sem.at[i]))
        stores[-1].start()
    for copy in copies[1:]:
        copy.wait()
    leaves, per_leaf = pos_ref.shape[1:]
    blank = jnp.zeros((1, lanes - leaves), jnp.int32)
    count = jnp.concatenate([counts_ref[...], blank], axis=1)
    count = jnp.broadcast_to(count, (lanes, lanes)).T[:leaves]
    point_at = lax.broadcasted_iota(jnp.int32, (leaves, per_leaf), 1)
    live = jnp.where(point_at < count, 1.0, 0.0)
    live_ref[...] = live
    for axis in range(3):
        packed_ref[axis] = pos_ref[axis]
        packed_ref[3 + axis] = frc_ref[axis] * live
    for store in stores:
        store.wait()


def near_field(
    slab_axis, neighbours_ref, live_ref, own_ref, even_ref, odd_ref, out_ref,
    point_ref, moment_ref, source_ref, weight_ref, target_wide_ref, target_ref, sums_ref, cube_ref,
):
    _, leaves, per_leaf = own_ref.shape
    group = 16
    pieces = 3
    nbr_count = neighbours_ref.shape[1]
    even = lax.rem(lax.axis_index(slab_axis), 2) == 0
    one = jnp.ones((leaves, per_leaf), f32)

    def stored(ref, leaf_start, height, rows):
        for row, value in enumerate(rows):
            ref[pl.ds(leaf_start * height + row, leaves, stride=height), :] = value

    def dot3(left, right):
        return left[0] * right[0] + left[1] * right[1] + left[2] * right[2]

    own_cut = None
    for part in range(3):
        if part == 0:
            comp = [jnp.where(even, odd_ref[c], even_ref[c]) for c in range(6)]
        elif part == 1:
            comp = [own_ref[c] for c in range(6)]
        else:
            comp = [jnp.where(even, even_ref[c], odd_ref[c]) for c in range(6)]
        cut = [split(c, 2) for c in comp[:3]]
        place = [high + low for high, low in cut]
        force = comp[3:]
        norm = dot3(place, place)
        along = dot3(force, place)
        size = split(norm + reg_eps2, 3)
        stored(point_ref, part * leaves, group, [c[0] for c in cut] + [c[1] for c in cut] + size)
        moments = force + [force[i] * place[j] for i in range(3) for j in range(3)]
        moments += [force[i] * (norm + 2.0 * reg_eps2) + along * place[i] for i in range(3)]
        stored(moment_ref, part * leaves, group, moments)
        if part == 1:
            own_cut, own_norm, own_place = cut, norm, place
    high = [-2.0 * c[0] for c in own_cut]
    low = [-2.0 * c[1] for c in own_cut]
    zero = jnp.zeros_like(one)
    rows = high + high + [one] * 3 + split(own_norm, 3) + [zero] * 4 + low + low + [zero] * 10
    stored(target_wide_ref, 0, 2 * group, rows)

    row_at = lax.broadcasted_iota(jnp.int32, (group, per_leaf), 0)
    def convert(leaf, carry):
        at = pl.ds(pl.multiple_of(leaf * group, group), group)
        point = jnp.where(row_at < 9, point_ref[at, :], jnp.where(row_at < 12, 1.0, 0.0))
        source_ref[at, :] = point.astype(bf16)
        moment = jnp.where(row_at < 15, moment_ref[at, :], 0.0)
        for i, piece in enumerate(split(moment, pieces)):
            to = pl.ds(pl.multiple_of((leaf * pieces + i) * group, group), group)
            weight_ref[to, :] = piece.astype(bf16)
        return carry

    def turn(leaf, carry):
        block = target_wide_ref[pl.ds(pl.multiple_of(leaf * 2 * group, group), 2 * group), :]
        to = pl.ds(pl.multiple_of(leaf * per_leaf, per_leaf), per_leaf)
        target_ref[to, :] = block.T.astype(bf16)
        return carry

    lax.fori_loop(0, 3 * leaves, convert, 0, unroll=8)
    lax.fori_loop(0, leaves, turn, 0, unroll=8)

    deep = pieces * group
    batch = cube_ref.shape[0] // 2

    def cubes(step):
        slot = lax.rem(step, 2) * batch
        for k in range(batch):
            leaf = step * batch + k
            target = target_ref[pl.ds(pl.multiple_of(leaf * per_leaf, per_leaf), per_leaf), :]
            for n in range(0, nbr_count, 2):
                near = [neighbours_ref[0, n + i, leaf] for i in range(2)]
                points = [source_ref[pl.ds(pl.multiple_of(i * group, group), group), :] for i in near]
                points = jnp.concatenate(points, axis=1)
                dist_sq = jnp.dot(
                    target, jnp.concatenate([points, points], axis=0), preferred_element_type=f32
                )
                inverse = lax.rsqrt(dist_sq)
                cube = (inverse * inverse * inverse).astype(bf16)
                cube_ref[slot + k, :, n * per_leaf : (n + 2) * per_leaf] = cube

    def sums(step):
        slot = lax.rem(step, 2) * batch
        for k in range(batch):
            leaf = step * batch + k
            near = [neighbours_ref[0, n, leaf] for n in range(nbr_count)]
            weights = [weight_ref[pl.ds(pl.multiple_of(i * deep, group), deep), :] for i in near]
            total = lax.dot_general(
                cube_ref[slot + k],
                jnp.concatenate(weights, axis=1),
                (((1,), (1,)), ((), ())),
                preferred_element_type=f32,
            ).T
            total = total[:group] + total[group : 2 * group] + total[2 * group :]
            sums_ref[pl.ds(leaf, group, stride=leaves), :] = total

    def both(step, carry):
        sums(step - 1)
        cubes(step)
        return carry

    steps = leaves // batch
    cubes(0)
    lax.fori_loop(1, steps, both, 0)
    sums(steps - 1)

    got = [sums_ref[pl.ds(row * leaves, leaves), :] for row in range(15)]
    first, mixed, rest = got[:3], [got[3 + 3 * i : 6 + 3 * i] for i in range(3)], got[12:]
    factor = live_ref[...] * inv_eight_pi
    shift = dot3(own_place, first) - (mixed[0][0] + mixed[1][1] + mixed[2][2])
    for i in range(3):
        turned = dot3(own_place, [2.0 * mixed[i][j] + mixed[j][i] for j in range(3)])
        out_ref[i] = (own_norm * first[i] + own_place[i] * shift - turned + rest[i]) * factor


def far_field(sources_ref, rows_ref, tile_of, out_ref, out_hbm, pick_ref, moved_ref, out_sem):
    coeffs, slot_count = out_ref.shape[0], rows_ref.shape[0]
    directions = pick_ref.shape[0] // slot_count
    tile = moved_ref.shape[1]
    octant = rows_ref[:, coeffs : coeffs + 2].astype(f32).astype(jnp.int32)
    octant = octant[:, :1] * id_base + octant[:, 1:]
    for t in range(directions):
        hit = octant == sources_ref[0, t : t + 1, :]
        pick_ref[t * slot_count : (t + 1) * slot_count, :] = jnp.where(hit, 1.0, 0.0).astype(bf16)
    rows = rows_ref[:, :coeffs]
    stores = []
    for i, start in enumerate(range(0, coeffs, tile)):
        ops_ref = tile_of(i)
        size = min(tile, coeffs - start)
        for t in range(directions):
            moved = jnp.dot(rows, ops_ref[t], preferred_element_type=f32)
            moved_ref[t * slot_count : (t + 1) * slot_count, :size] = moved.astype(bf16)
        for low in range(0, size, 2 * lanes):
            rest = min(2 * lanes, size - low)
            total = lax.dot_general(
                moved_ref[:, low : low + rest],
                pick_ref[...],
                (((0,), (0,)), ((), ())),
                preferred_element_type=f32,
            )
            at = pl.ds(start + low, rest)
            out_ref[at, :] = total.astype(bf16)
            sem = out_sem.at[len(stores)]
            stores.append(pltpu.make_async_copy(out_ref.at[at, :], out_hbm.at[at, :], sem))
            stores[-1].start()
    return stores


def near_kernel(
    slab_axis, neighbours_ref, live_ref, own_ref, odd_ref, even_ref, ops_hbm,
    velocity_ref, head_ref,
    point_ref, moment_ref, source_ref, weight_ref, target_wide_ref, target_ref, sums_ref, cube_ref, sem,
):
    head = pltpu.make_async_copy(ops_hbm.at[:, :, pl.ds(0, head_ref.shape[2])], head_ref, sem)
    head.start()
    near_field(
        slab_axis, neighbours_ref, live_ref, own_ref, even_ref, odd_ref, velocity_ref,
        point_ref, moment_ref, source_ref, weight_ref, target_wide_ref, target_ref, sums_ref, cube_ref,
    )
    head.wait()


def far_kernel(
    picks_ref, rows_ref, head_ref, velocity_ref, ops_hbm, local_hbm, velocity_hbm,
    ops_ref, pick_ref, moved_ref, local_ref, ops_sem, out_sem,
):
    coeffs, tile = ops_hbm.shape[1], moved_ref.shape[1]
    loads = [None]
    for i, start in enumerate(range(tile, coeffs, tile)):
        at = pl.ds(start, min(tile, coeffs - start))
        loads.append(pltpu.make_async_copy(ops_hbm.at[:, :, at], ops_ref.at[:, :, at], ops_sem.at[i]))
        loads[-1].start()

    velocity_store = pltpu.make_async_copy(velocity_ref, velocity_hbm, ops_sem.at[len(loads) - 1])
    velocity_store.start()

    def tile_of(i):
        if i == 0:
            return head_ref
        loads[i].wait()
        return ops_ref.at[:, :, pl.ds(i * tile, min(tile, coeffs - i * tile))]

    stores = far_field(picks_ref, rows_ref, tile_of, local_ref, local_hbm, pick_ref, moved_ref, out_sem)
    for store in stores + [velocity_store]:
        store.wait()


def vmem():
    return pl.BlockSpec(memory_space=pltpu.VMEM)


def in_hbm(array):
    return pltpu.with_memory_space_constraint(array, pltpu.HBM)


def smem():
    return pl.BlockSpec(memory_space=pltpu.SMEM)


def hbm():
    return pl.BlockSpec(memory_space=pltpu.HBM)


def call_near(neighbours, live, packed, odd, even, m2l_ops, tile):
    _, leaves, per_leaf = packed.shape
    directions, coeffs, _ = m2l_ops.shape
    table = 3 * leaves
    return pl.pallas_call(
        functools.partial(near_kernel, "nb"),
        out_shape=(
            pltpu.VMEM((3, leaves, per_leaf), f32),
            pltpu.VMEM((directions, coeffs, tile), bf16),
        ),
        in_specs=[smem()] + [vmem()] * 4 + [hbm()],
        out_specs=(vmem(), vmem()),
        scratch_shapes=[
            pltpu.VMEM((table * 16, per_leaf), f32),
            pltpu.VMEM((table * 16, per_leaf), f32),
            pltpu.VMEM((table * 16, per_leaf), bf16),
            pltpu.VMEM((table * 48, per_leaf), bf16),
            pltpu.VMEM((leaves * 32, per_leaf), f32),
            pltpu.VMEM((leaves * per_leaf, 32), bf16),
            pltpu.VMEM((16 * leaves, per_leaf), f32),
            pltpu.VMEM((2 * 8, per_leaf, neighbours.shape[1] * per_leaf), bf16),
            pltpu.SemaphoreType.DMA,
        ],
        compiler_params=pltpu.CompilerParams(vmem_limit_bytes=24 * 2**20),
        name="near",
    )(neighbours, live, packed, odd, even, in_hbm(m2l_ops))


def call_far(m2l_sources, arrived, head, velocity, m2l_ops):
    directions, coeffs, tile = head.shape
    owned = m2l_sources.shape[2]
    picks = directions * arrived.shape[0]
    return pl.pallas_call(
        far_kernel,
        out_shape=(
            jax.ShapeDtypeStruct((coeffs, owned), bf16),
            jax.ShapeDtypeStruct(velocity.shape, f32),
        ),
        in_specs=[vmem()] * 4 + [hbm()],
        out_specs=(hbm(), hbm()),
        scratch_shapes=[
            pltpu.VMEM(m2l_ops.shape, bf16),
            pltpu.VMEM((picks, owned), bf16),
            pltpu.VMEM((picks, tile), bf16),
            pltpu.VMEM((coeffs, owned), bf16),
            pltpu.SemaphoreType.DMA((-(-coeffs // tile),)),
            pltpu.SemaphoreType.DMA((-(-coeffs // (2 * lanes)),)),
        ],
        compiler_params=pltpu.CompilerParams(vmem_limit_bytes=40 * 2**20),
        name="far",
    )(m2l_sources, arrived, head, velocity, in_hbm(m2l_ops))


def call_presum(hx_count, partial_multipoles, shared_slots, positions, forces, leaf_counts, neighbours):
    row_count, coeffs = partial_multipoles.shape[1:]
    cap = row_count // hx_count
    uniq = cap // 4
    slot_count = hx_count * uniq
    width = -(-(coeffs + 2) // lanes) * lanes
    tile = width
    steps = -(-coeffs // tile)
    leaves = leaf_counts.shape[1]
    per_leaf = positions.shape[2] // leaves

    return pl.pallas_call(
        functools.partial(presum_kernel, cap, uniq, tile),
        out_shape=(
            jax.ShapeDtypeStruct((slot_count, width), bf16),
            pltpu.VMEM((6, leaves, per_leaf), f32),
            pltpu.VMEM((leaves, per_leaf), f32),
            pltpu.SMEM(neighbours.shape, jnp.int32),
        ),
        in_specs=[hbm()] * 6,
        out_specs=(hbm(), vmem(), vmem(), smem()),
        scratch_shapes=[
            pltpu.VMEM(leaf_counts.shape, jnp.int32),
            pltpu.VMEM(shared_slots.shape, jnp.int32),
            pltpu.VMEM((coeffs, row_count), bf16),
            pltpu.VMEM((3, leaves, per_leaf), f32),
            pltpu.VMEM((3, leaves, per_leaf), f32),
            pltpu.VMEM((slot_count, width), bf16),
            pltpu.SemaphoreType.DMA((5,)),
            pltpu.SemaphoreType.DMA((steps,)),
            pltpu.SemaphoreType.DMA((steps,)),
        ],
        compiler_params=pltpu.CompilerParams(vmem_limit_bytes=16 * 2**20),
        name="presum",
    )(
        *map(
            in_hbm,
            (
                leaf_counts,
                shared_slots,
                partial_multipoles[0].T,
                positions[0].reshape(3, leaves, per_leaf),
                forces[0].reshape(3, leaves, per_leaf),
                neighbours,
            ),
        )
    )


def on_device(
    partial_multipoles,
    shared_slots,
    m2l_sources,
    m2l_ops,
    positions,
    forces,
    leaf_counts,
    neighbours,
):
    hx_count, nb_count = lax.axis_size("hx"), lax.axis_size("nb")
    sums, packed, live, sources = call_presum(
        hx_count, partial_multipoles, shared_slots, positions, forces, leaf_counts, neighbours
    )

    even_pairs = [(i, i + 1) for i in range(0, nb_count - 1, 2)]
    odd_pairs = [(i, i + 1) for i in range(1, nb_count - 1, 2)]
    even = lax.ppermute(packed, "nb", even_pairs + [(j, i) for i, j in even_pairs])
    odd = lax.ppermute(packed, "nb", odd_pairs + [(j, i) for i, j in odd_pairs])
    arrived = lax.all_to_all(
        sums.reshape(hx_count, -1, sums.shape[1]), "hx", split_axis=0, concat_axis=0, tiled=True
    ).reshape(sums.shape)

    velocity, head = call_near(sources, live, packed, odd, even, m2l_ops, 4 * lanes)
    local, velocity = call_far(m2l_sources, arrived, head, velocity, m2l_ops)

    return local.T[None], velocity.reshape(positions.shape)


def solution(mesh):
    placed = (
        P("nb", "hx", None),
        P("nb", "hx"),
        P("nb", None, "hx"),
        P(),
        P("nb", None, "hx"),
        P("nb", None, "hx"),
        P("nb", "hx"),
        P("nb", None, "hx"),
    )
    return jax.shard_map(
        on_device,
        mesh=mesh,
        in_specs=placed,
        out_specs=(P("nb", "hx", None), P("nb", None, "hx")),
        check_vma=False,
    )
```

```python
import functools
import math

import jax
import jax.numpy as jnp
from jax import lax
from jax.experimental import pallas as pl
from jax.experimental.pallas import tpu as pltpu
from jax.sharding import PartitionSpec as P

reg_eps2 = 0.01
inv_eight_pi = 1.0 / (8.0 * math.pi)
id_base = 32
lanes = 128
group = 16
pieces = 3
bf16 = jnp.bfloat16
f32 = jnp.float32


def split(value, count):
    pieces = []
    for _ in range(count):
        piece = value.astype(bf16).astype(f32)
        pieces.append(piece)
        value = value - piece
    return pieces


def presum_kernel(
    cap, uniq, tile, counts_hbm, slots_hbm, rows_hbm, pos_hbm, frc_hbm, neighbours_hbm,
    sums_hbm, packed_ref, live_ref, neighbours_out,
    counts_ref, slots_ref, rows_ref, pos_ref, frc_ref, sums_ref, arrival, rows_sem, sums_sem,
):
    coeffs, row_count = rows_ref.shape
    slot_count, width = sums_ref.shape
    spans = [(start, min(tile, coeffs - start)) for start in range(0, coeffs, tile)]
    pairs = (
        (slots_hbm, slots_ref),
        (counts_hbm, counts_ref),
        (pos_hbm, pos_ref),
        (frc_hbm, frc_ref),
        (neighbours_hbm, neighbours_out),
    )
    copies = [pltpu.make_async_copy(a, b, arrival.at[i]) for i, (a, b) in enumerate(pairs)]
    loads = []
    for i, (start, size) in enumerate(spans):
        at = pl.ds(start, size)
        loads.append(pltpu.make_async_copy(rows_hbm.at[at, :], rows_ref.at[at, :], rows_sem.at[i]))
    for copy in copies[:1] + loads + copies[1:]:
        copy.start()
    copies[0].wait()

    targets = []
    sub_at = lax.broadcasted_iota(jnp.int32, (lanes, lanes), 0)
    lane_at = lax.broadcasted_iota(jnp.int32, (lanes, lanes), 1)
    same_block = (sub_at // cap) == (lane_at // cap)
    for start in range(0, row_count, lanes):
        by_lane = jnp.broadcast_to(slots_ref[:, start : start + lanes], (lanes, lanes))
        by_sub = by_lane.T
        equal = same_block & (by_lane == by_sub)
        seen = jnp.where(equal & (lane_at < sub_at), 1, 0)
        first = (jnp.max(seen, axis=1, keepdims=True) == 0) & (by_sub >= 0)
        below = jnp.where(first & same_block & (by_sub < by_lane), 1, 0)
        rank = jnp.sum(below, axis=0, keepdims=True)
        lane_row = lax.broadcasted_iota(jnp.int32, (1, lanes), 1) + start
        block = lane_row // cap
        valid = slots_ref[:, start : start + lanes] >= 0
        targets.append(jnp.where(valid, block * uniq + rank, -1))
    target = jnp.concatenate(targets, axis=1)
    slot_at = lax.broadcasted_iota(jnp.int32, (slot_count, row_count), 0)
    hit = slot_at == target
    octant = jnp.max(jnp.where(hit, slots_ref[...], -1), axis=1, keepdims=True)
    one_hot = jnp.where(hit, 1.0, 0.0).astype(bf16)
    high = octant // id_base
    low = octant - high * id_base
    extra_at = lax.broadcasted_iota(jnp.int32, (slot_count, width - coeffs), 1)
    extra = jnp.where(extra_at == 0, high, jnp.where(extra_at == 1, low, 0))
    sums_ref[:, coeffs:] = extra.astype(f32).astype(bf16)
    stores = []
    for i, (start, size) in enumerate(spans):
        loads[i].wait()
        sums = lax.dot_general(
            one_hot,
            rows_ref[start : start + size, :],
            (((1,), (1,)), ((), ())),
            preferred_element_type=f32,
        )
        sums_ref[:, start : start + size] = sums.astype(bf16)
        at = pl.ds(start, min(tile, width - start))
        stores.append(pltpu.make_async_copy(sums_ref.at[:, at], sums_hbm.at[:, at], sums_sem.at[i]))
        stores[-1].start()
    for copy in copies[1:]:
        copy.wait()
    leaves, per_leaf = pos_ref.shape[1:]
    blank = jnp.zeros((1, lanes - leaves), jnp.int32)
    count = jnp.concatenate([counts_ref[...], blank], axis=1)
    count = jnp.broadcast_to(count, (lanes, lanes)).T[:leaves]
    point_at = lax.broadcasted_iota(jnp.int32, (leaves, per_leaf), 1)
    live = jnp.where(point_at < count, 1.0, 0.0)
    live_ref[...] = live
    for axis in range(3):
        packed_ref[axis] = pos_ref[axis]
        packed_ref[3 + axis] = frc_ref[axis] * live
    for store in stores:
        store.wait()


def dot3(left, right):
    return left[0] * right[0] + left[1] * right[1] + left[2] * right[2]


def near_tables(
    slab_axis, own_ref, even_ref, odd_ref, point_ref, moment_ref, target_wide_ref, source_ref, weight_ref
):
    _, leaves, per_leaf = own_ref.shape
    even = lax.rem(lax.axis_index(slab_axis), 2) == 0

    def stored(ref, leaf_start, height, rows):
        for row, value in enumerate(rows):
            ref[pl.ds(leaf_start * height + row, leaves, stride=height), :] = value

    for part in range(3):
        if part == 0:
            comp = [jnp.where(even, odd_ref[c], even_ref[c]) for c in range(6)]
        elif part == 1:
            comp = [own_ref[c] for c in range(6)]
        else:
            comp = [jnp.where(even, even_ref[c], odd_ref[c]) for c in range(6)]
        cut = [split(c, 2) for c in comp[:3]]
        place = [high + low for high, low in cut]
        force = comp[3:]
        norm = dot3(place, place)
        along = dot3(force, place)
        size = split(norm + reg_eps2, 3)
        stored(point_ref, part * leaves, group, [c[0] for c in cut] + [c[1] for c in cut] + size)
        moments = force + [force[i] * place[j] for i in range(3) for j in range(3)]
        moments += [force[i] * (norm + 2.0 * reg_eps2) + along * place[i] for i in range(3)]
        stored(moment_ref, part * leaves, group, moments)
        if part == 1:
            zero, one = jnp.zeros_like(norm), jnp.ones_like(norm)
            high = [-2.0 * c[0] for c in cut]
            low = [-2.0 * c[1] for c in cut]
            rows = high + high + [one] * 3 + split(norm, 3) + [zero] * 4 + low + low + [zero] * 10
            stored(target_wide_ref, 0, 2 * group, rows)

    row_at = lax.broadcasted_iota(jnp.int32, (group, per_leaf), 0)

    def convert(leaf, carry):
        at = pl.ds(pl.multiple_of(leaf * group, group), group)
        point = jnp.where(row_at < 9, point_ref[at, :], jnp.where(row_at < 12, 1.0, 0.0))
        source_ref[at, :] = point.astype(bf16)
        moment = jnp.where(row_at < 15, moment_ref[at, :], 0.0)
        for i, piece in enumerate(split(moment, pieces)):
            to = pl.ds(pl.multiple_of((leaf * pieces + i) * group, group), group)
            weight_ref[to, :] = piece.astype(bf16)
        return carry

    lax.fori_loop(0, 3 * leaves, convert, 0, unroll=8)


def near_leaves(
    first, neighbours_ref, own_ref, live, target_wide_ref,
    source_ref, weight_ref, target_ref, cube_ref, sums_ref, out_ref,
):
    count, per_leaf = live.shape
    height = 2 * group
    nbr_count = neighbours_ref.shape[1]
    deep = pieces * group
    for k in range(count):
        wide = target_wide_ref[(first + k) * height : (first + k + 1) * height, :]
        target_ref[k * per_leaf : (k + 1) * per_leaf, :] = wide.T.astype(bf16)
    for k in range(count):
        target = target_ref[k * per_leaf : (k + 1) * per_leaf, :]
        for n in range(0, nbr_count, 2):
            near = [neighbours_ref[0, n + i, first + k] for i in range(2)]
            points = [source_ref[pl.ds(pl.multiple_of(i * group, group), group), :] for i in near]
            points = jnp.concatenate(points, axis=1)
            dist_sq = jnp.dot(
                target, jnp.concatenate([points, points], axis=0), preferred_element_type=f32
            )
            inverse = lax.rsqrt(dist_sq)
            cube = (inverse * inverse * inverse).astype(bf16)
            cube_ref[k, :, n * per_leaf : (n + 2) * per_leaf] = cube
    for k in range(count):
        near = [neighbours_ref[0, n, first + k] for n in range(nbr_count)]
        weights = [weight_ref[pl.ds(pl.multiple_of(i * deep, group), deep), :] for i in near]
        total = lax.dot_general(
            cube_ref[k],
            jnp.concatenate(weights, axis=1),
            (((1,), (1,)), ((), ())),
            preferred_element_type=f32,
        ).T
        total = total[:group] + total[group : 2 * group] + total[2 * group :]
        sums_ref[pl.ds(k, group, stride=count), :] = total

    got = [sums_ref[row * count : (row + 1) * count, :] for row in range(15)]
    start, mixed, rest = got[:3], [got[3 + 3 * i : 6 + 3 * i] for i in range(3)], got[12:]
    place = [sum(split(own_ref[axis, first : first + count, :], 2)) for axis in range(3)]
    norm = dot3(place, place)
    factor = live * inv_eight_pi
    shift = dot3(place, start) - (mixed[0][0] + mixed[1][1] + mixed[2][2])
    for i in range(3):
        turned = dot3(place, [2.0 * mixed[i][j] + mixed[j][i] for j in range(3)])
        out_ref[i] = (norm * start[i] + place[i] * shift - turned + rest[i]) * factor


def far_field(sources_ref, rows_ref, tile_of, out_ref, out_hbm, pick_ref, moved_ref, out_sem):
    coeffs, slot_count = out_ref.shape[0], rows_ref.shape[0]
    directions = pick_ref.shape[0] // slot_count
    tile = moved_ref.shape[1]
    octant = rows_ref[:, coeffs : coeffs + 2].astype(f32).astype(jnp.int32)
    octant = octant[:, :1] * id_base + octant[:, 1:]
    for t in range(directions):
        hit = octant == sources_ref[0, t : t + 1, :]
        pick_ref[t * slot_count : (t + 1) * slot_count, :] = jnp.where(hit, 1.0, 0.0).astype(bf16)
    rows = rows_ref[:, :coeffs]
    stores = []
    for i, start in enumerate(range(0, coeffs, tile)):
        parts = tile_of(i)
        size = min(tile, coeffs - start)
        for t in range(directions):
            deep = parts[0].shape[1]
            moved = jnp.dot(rows[:, :deep], parts[0][t], preferred_element_type=f32)
            if deep < coeffs:
                moved += jnp.dot(rows[:, deep:], parts[1][t], preferred_element_type=f32)
            moved_ref[t * slot_count : (t + 1) * slot_count, :size] = moved.astype(bf16)
        for low in range(0, size, 2 * lanes):
            rest = min(2 * lanes, size - low)
            total = lax.dot_general(
                moved_ref[:, low : low + rest],
                pick_ref[...],
                (((0,), (0,)), ((), ())),
                preferred_element_type=f32,
            )
            at = pl.ds(start + low, rest)
            out_ref[at, :] = total.astype(bf16)
            sem = out_sem.at[len(stores)]
            stores.append(pltpu.make_async_copy(out_ref.at[at, :], out_hbm.at[at, :], sem))
            stores[-1].start()
    return stores


def near_kernel(
    slab_axis, neighbours_ref, live_ref, own_ref, odd_ref, even_ref, ops_hbm,
    early_ref, head_ref,
    point_ref, moment_ref, target_wide_ref, source_ref, weight_ref, target_ref, cube_ref, sums_ref, sem,
):
    at = (slice(None), pl.ds(0, head_ref.shape[1]), pl.ds(0, head_ref.shape[2]))
    head = pltpu.make_async_copy(ops_hbm.at[at], head_ref, sem)
    head.start()
    near_tables(
        slab_axis, own_ref, even_ref, odd_ref,
        point_ref, moment_ref, target_wide_ref, source_ref, weight_ref,
    )
    count = early_ref.shape[1]
    near_leaves(
        0, neighbours_ref, own_ref, live_ref[:count, :], target_wide_ref,
        source_ref, weight_ref, target_ref, cube_ref, sums_ref, early_ref,
    )
    early_ref[3] = live_ref[count:, :]
    head.wait()


def far_kernel(
    slab_axis, neighbours_ref, own_ref, odd_ref, even_ref, picks_ref, rows_ref, head_ref, early_ref,
    ops_hbm, local_hbm, velocity_hbm,
    point_ref, moment_ref, target_wide_ref, source_ref, weight_ref, target_ref, cube_ref, sums_ref,
    ops_ref, pick_ref, moved_ref, local_ref, late_ref, velocity_ref, ops_sem, out_sem,
):
    coeffs, tile = ops_hbm.shape[1], moved_ref.shape[1]
    deep = head_ref.shape[1]
    rest = (slice(None), pl.ds(deep, coeffs - deep), pl.ds(0, tile))
    loads = [pltpu.make_async_copy(ops_hbm.at[rest], ops_ref.at[rest], ops_sem.at[0])]
    loads[0].start()
    for i, start in enumerate(range(tile, coeffs, tile)):
        at = pl.ds(start, min(tile, coeffs - start))
        loads.append(pltpu.make_async_copy(ops_hbm.at[:, :, at], ops_ref.at[:, :, at], ops_sem.at[i + 1]))
        loads[-1].start()

    count = early_ref.shape[1]
    near_tables(
        slab_axis, own_ref, even_ref, odd_ref,
        point_ref, moment_ref, target_wide_ref, source_ref, weight_ref,
    )
    near_leaves(
        count, neighbours_ref, own_ref, early_ref[3], target_wide_ref,
        source_ref, weight_ref, target_ref, cube_ref, sums_ref, late_ref,
    )
    for axis in range(3):
        velocity_ref[axis, :count, :] = early_ref[axis]
        velocity_ref[axis, count:, :] = late_ref[axis]
    velocity_store = pltpu.make_async_copy(velocity_ref, velocity_hbm, ops_sem.at[len(loads)])
    velocity_store.start()

    def tile_of(i):
        loads[i].wait()
        if i == 0:
            return (head_ref, ops_ref.at[rest])
        return (ops_ref.at[:, :, pl.ds(i * tile, min(tile, coeffs - i * tile))],)

    stores = far_field(picks_ref, rows_ref, tile_of, local_ref, local_hbm, pick_ref, moved_ref, out_sem)
    for store in stores + [velocity_store]:
        store.wait()


def vmem():
    return pl.BlockSpec(memory_space=pltpu.VMEM)


def in_hbm(array):
    return pltpu.with_memory_space_constraint(array, pltpu.HBM)


def smem():
    return pl.BlockSpec(memory_space=pltpu.SMEM)


def hbm():
    return pl.BlockSpec(memory_space=pltpu.HBM)


def near_scratch(neighbours, packed):
    _, leaves, per_leaf = packed.shape
    table, count = 3 * leaves, leaves // 2
    return [
        pltpu.VMEM((table * group, per_leaf), f32),
        pltpu.VMEM((table * group, per_leaf), f32),
        pltpu.VMEM((leaves * 2 * group, per_leaf), f32),
        pltpu.VMEM((table * group, per_leaf), bf16),
        pltpu.VMEM((table * pieces * group, per_leaf), bf16),
        pltpu.VMEM((count * per_leaf, 2 * group), bf16),
        pltpu.VMEM((count, per_leaf, neighbours.shape[1] * per_leaf), bf16),
        pltpu.VMEM((group * count, per_leaf), f32),
    ]


def call_near(neighbours, live, packed, odd, even, m2l_ops, tile):
    _, leaves, per_leaf = packed.shape
    directions, coeffs, _ = m2l_ops.shape
    return pl.pallas_call(
        functools.partial(near_kernel, "nb"),
        out_shape=(
            pltpu.VMEM((4, leaves // 2, per_leaf), f32),
            pltpu.VMEM((directions, coeffs // lanes * lanes, tile), bf16),
        ),
        in_specs=[smem()] + [vmem()] * 4 + [hbm()],
        out_specs=(vmem(), vmem()),
        scratch_shapes=near_scratch(neighbours, packed) + [pltpu.SemaphoreType.DMA],
        compiler_params=pltpu.CompilerParams(vmem_limit_bytes=24 * 2**20),
        name="near",
    )(neighbours, live, packed, odd, even, in_hbm(m2l_ops))


def call_far(neighbours, packed, odd, even, m2l_sources, arrived, head, early, m2l_ops):
    _, leaves, per_leaf = packed.shape
    directions, coeffs, _ = m2l_ops.shape
    tile = head.shape[2]
    owned = m2l_sources.shape[2]
    picks = directions * arrived.shape[0]
    steps = -(-coeffs // tile)
    return pl.pallas_call(
        functools.partial(far_kernel, "nb"),
        out_shape=(
            jax.ShapeDtypeStruct((coeffs, owned), bf16),
            jax.ShapeDtypeStruct((3, leaves, per_leaf), f32),
        ),
        in_specs=[smem()] + [vmem()] * 7 + [hbm()],
        out_specs=(hbm(), hbm()),
        scratch_shapes=near_scratch(neighbours, packed)
        + [
            pltpu.VMEM(m2l_ops.shape, bf16),
            pltpu.VMEM((picks, owned), bf16),
            pltpu.VMEM((picks, tile), bf16),
            pltpu.VMEM((coeffs, owned), bf16),
            pltpu.VMEM((3, leaves - leaves // 2, per_leaf), f32),
            pltpu.VMEM((3, leaves, per_leaf), f32),
            pltpu.SemaphoreType.DMA((steps + 1,)),
            pltpu.SemaphoreType.DMA((2 * steps,)),
        ],
        compiler_params=pltpu.CompilerParams(vmem_limit_bytes=40 * 2**20),
        name="far",
    )(neighbours, packed, odd, even, m2l_sources, arrived, head, early, in_hbm(m2l_ops))


def call_presum(hx_count, partial_multipoles, shared_slots, positions, forces, leaf_counts, neighbours):
    row_count, coeffs = partial_multipoles.shape[1:]
    cap = row_count // hx_count
    uniq = cap // 4
    slot_count = hx_count * uniq
    width = -(-(coeffs + 2) // lanes) * lanes
    tile = width
    steps = -(-coeffs // tile)
    leaves = leaf_counts.shape[1]
    per_leaf = positions.shape[2] // leaves

    return pl.pallas_call(
        functools.partial(presum_kernel, cap, uniq, tile),
        out_shape=(
            jax.ShapeDtypeStruct((slot_count, width), bf16),
            pltpu.VMEM((6, leaves, per_leaf), f32),
            pltpu.VMEM((leaves, per_leaf), f32),
            pltpu.SMEM(neighbours.shape, jnp.int32),
        ),
        in_specs=[hbm()] * 6,
        out_specs=(hbm(), vmem(), vmem(), smem()),
        scratch_shapes=[
            pltpu.VMEM(leaf_counts.shape, jnp.int32),
            pltpu.VMEM(shared_slots.shape, jnp.int32),
            pltpu.VMEM((coeffs, row_count), bf16),
            pltpu.VMEM((3, leaves, per_leaf), f32),
            pltpu.VMEM((3, leaves, per_leaf), f32),
            pltpu.VMEM((slot_count, width), bf16),
            pltpu.SemaphoreType.DMA((5,)),
            pltpu.SemaphoreType.DMA((steps,)),
            pltpu.SemaphoreType.DMA((steps,)),
        ],
        compiler_params=pltpu.CompilerParams(vmem_limit_bytes=16 * 2**20),
        name="presum",
    )(
        *map(
            in_hbm,
            (
                leaf_counts,
                shared_slots,
                partial_multipoles[0].T,
                positions[0].reshape(3, leaves, per_leaf),
                forces[0].reshape(3, leaves, per_leaf),
                neighbours,
            ),
        )
    )


def on_device(
    partial_multipoles,
    shared_slots,
    m2l_sources,
    m2l_ops,
    positions,
    forces,
    leaf_counts,
    neighbours,
):
    hx_count, nb_count = lax.axis_size("hx"), lax.axis_size("nb")
    sums, packed, live, sources = call_presum(
        hx_count, partial_multipoles, shared_slots, positions, forces, leaf_counts, neighbours
    )

    even_pairs = [(i, i + 1) for i in range(0, nb_count - 1, 2)]
    odd_pairs = [(i, i + 1) for i in range(1, nb_count - 1, 2)]
    even = lax.ppermute(packed, "nb", even_pairs + [(j, i) for i, j in even_pairs])
    odd = lax.ppermute(packed, "nb", odd_pairs + [(j, i) for i, j in odd_pairs])
    arrived = lax.all_to_all(
        sums.reshape(hx_count, -1, sums.shape[1]), "hx", split_axis=0, concat_axis=0, tiled=True
    ).reshape(sums.shape)

    early, head = call_near(sources, live, packed, odd, even, m2l_ops, 4 * lanes)
    local, velocity = call_far(
        sources, packed, odd, even, m2l_sources, arrived, head, early, m2l_ops
    )

    return local.T[None], velocity.reshape(positions.shape)


def solution(mesh):
    placed = (
        P("nb", "hx", None),
        P("nb", "hx"),
        P("nb", None, "hx"),
        P(),
        P("nb", None, "hx"),
        P("nb", None, "hx"),
        P("nb", "hx"),
        P("nb", None, "hx"),
    )
    return jax.shard_map(
        on_device,
        mesh=mesh,
        in_specs=placed,
        out_specs=(P("nb", "hx", None), P("nb", None, "hx")),
        check_vma=False,
    )
```

```python
import functools
import math

import jax
import jax.numpy as jnp
from jax import lax
from jax.experimental import pallas as pl
from jax.experimental.pallas import tpu as pltpu
from jax.sharding import PartitionSpec as P

reg_eps2 = 0.01
inv_eight_pi = 1.0 / (8.0 * math.pi)
id_base = 32
lanes = 128
group = 16
pieces = 3
bf16 = jnp.bfloat16
f32 = jnp.float32


def split(value, count):
    pieces = []
    for _ in range(count):
        piece = value.astype(bf16).astype(f32)
        pieces.append(piece)
        value = value - piece
    return pieces


def presum_kernel(
    cap, uniq, tile, counts_hbm, slots_hbm, rows_hbm, pos_hbm, frc_hbm, neighbours_hbm,
    sums_hbm, packed_ref, sent_ref, live_ref, neighbours_out,
    counts_ref, slots_ref, rows_ref, pos_ref, frc_ref, sums_ref, arrival, rows_sem, sums_sem,
):
    coeffs, row_count = rows_ref.shape
    slot_count, width = sums_ref.shape
    spans = [(start, min(tile, coeffs - start)) for start in range(0, coeffs, tile)]
    pairs = (
        (slots_hbm, slots_ref),
        (counts_hbm, counts_ref),
        (pos_hbm, pos_ref),
        (frc_hbm, frc_ref),
        (neighbours_hbm, neighbours_out),
    )
    copies = [pltpu.make_async_copy(a, b, arrival.at[i]) for i, (a, b) in enumerate(pairs)]
    loads = []
    for i, (start, size) in enumerate(spans):
        at = pl.ds(start, size)
        loads.append(pltpu.make_async_copy(rows_hbm.at[at, :], rows_ref.at[at, :], rows_sem.at[i]))
    for copy in copies[:1] + loads + copies[1:]:
        copy.start()
    copies[0].wait()

    targets = []
    sub_at = lax.broadcasted_iota(jnp.int32, (lanes, lanes), 0)
    lane_at = lax.broadcasted_iota(jnp.int32, (lanes, lanes), 1)
    same_block = (sub_at // cap) == (lane_at // cap)
    for start in range(0, row_count, lanes):
        by_lane = jnp.broadcast_to(slots_ref[:, start : start + lanes], (lanes, lanes))
        by_sub = by_lane.T
        equal = same_block & (by_lane == by_sub)
        seen = jnp.where(equal & (lane_at < sub_at), 1, 0)
        first = (jnp.max(seen, axis=1, keepdims=True) == 0) & (by_sub >= 0)
        below = jnp.where(first & same_block & (by_sub < by_lane), 1, 0)
        rank = jnp.sum(below, axis=0, keepdims=True)
        lane_row = lax.broadcasted_iota(jnp.int32, (1, lanes), 1) + start
        block = lane_row // cap
        valid = slots_ref[:, start : start + lanes] >= 0
        targets.append(jnp.where(valid, block * uniq + rank, -1))
    target = jnp.concatenate(targets, axis=1)
    slot_at = lax.broadcasted_iota(jnp.int32, (slot_count, row_count), 0)
    hit = slot_at == target
    octant = jnp.max(jnp.where(hit, slots_ref[...], -1), axis=1, keepdims=True)
    one_hot = jnp.where(hit, 1.0, 0.0).astype(bf16)
    high = octant // id_base
    low = octant - high * id_base
    extra_at = lax.broadcasted_iota(jnp.int32, (slot_count, width - coeffs), 1)
    extra = jnp.where(extra_at == 0, high, jnp.where(extra_at == 1, low, 0))
    sums_ref[:, coeffs:] = extra.astype(f32).astype(bf16)
    stores = []
    for i, (start, size) in enumerate(spans):
        loads[i].wait()
        sums = lax.dot_general(
            one_hot,
            rows_ref[start : start + size, :],
            (((1,), (1,)), ((), ())),
            preferred_element_type=f32,
        )
        sums_ref[:, start : start + size] = sums.astype(bf16)
        at = pl.ds(start, min(tile, width - start))
        stores.append(pltpu.make_async_copy(sums_ref.at[:, at], sums_hbm.at[:, at], sums_sem.at[i]))
        stores[-1].start()
    for copy in copies[1:]:
        copy.wait()
    leaves, per_leaf = pos_ref.shape[1:]
    blank = jnp.zeros((1, lanes - leaves), jnp.int32)
    count = jnp.concatenate([counts_ref[...], blank], axis=1)
    count = jnp.broadcast_to(count, (lanes, lanes)).T[:leaves]
    point_at = lax.broadcasted_iota(jnp.int32, (leaves, per_leaf), 1)
    live = jnp.where(point_at < count, 1.0, 0.0)
    live_ref[...] = live
    for axis in range(3):
        masked = frc_ref[axis] * live
        packed_ref[axis] = pos_ref[axis]
        packed_ref[3 + axis] = masked
        high, low = split(pos_ref[axis], 2)
        for row, value in enumerate((high, low, masked)):
            sent_ref[3 * row + axis] = value.astype(bf16)
    for store in stores:
        store.wait()


def dot3(left, right):
    return left[0] * right[0] + left[1] * right[1] + left[2] * right[2]


def near_tables(
    slab_axis, own_ref, even_ref, odd_ref, point_ref, moment_ref, target_wide_ref, source_ref, weight_ref
):
    _, leaves, per_leaf = own_ref.shape
    even = lax.rem(lax.axis_index(slab_axis), 2) == 0

    def stored(ref, leaf_start, height, rows):
        for row, value in enumerate(rows):
            ref[pl.ds(leaf_start * height + row, leaves, stride=height), :] = value

    for part in range(3):
        if part == 1:
            cut = [split(own_ref[c], 2) for c in range(3)]
            force = [own_ref[3 + c] for c in range(3)]
        else:
            refs = (odd_ref, even_ref) if part == 0 else (even_ref, odd_ref)
            comp = [jnp.where(even, refs[0][c], refs[1][c]).astype(f32) for c in range(9)]
            cut = [comp[c : c + 4 : 3] for c in range(3)]
            force = comp[6:]
        place = [high + low for high, low in cut]
        norm = dot3(place, place)
        along = dot3(force, place)
        size = split(norm + reg_eps2, 3)
        stored(point_ref, part * leaves, group, [c[0] for c in cut] + [c[1] for c in cut] + size)
        moments = force + [force[i] * place[j] for i in range(3) for j in range(3)]
        moments += [force[i] * (norm + 2.0 * reg_eps2) + along * place[i] for i in range(3)]
        stored(moment_ref, part * leaves, group, moments)
        if part == 1:
            zero, one = jnp.zeros_like(norm), jnp.ones_like(norm)
            high = [-2.0 * c[0] for c in cut]
            low = [-2.0 * c[1] for c in cut]
            rows = high + high + [one] * 3 + split(norm, 3) + [zero] * 4 + low + low + [zero] * 10
            stored(target_wide_ref, 0, 2 * group, rows)

    row_at = lax.broadcasted_iota(jnp.int32, (group, per_leaf), 0)

    def convert(leaf, carry):
        at = pl.ds(pl.multiple_of(leaf * group, group), group)
        point = jnp.where(row_at < 9, point_ref[at, :], jnp.where(row_at < 12, 1.0, 0.0))
        source_ref[at, :] = point.astype(bf16)
        moment = jnp.where(row_at < 15, moment_ref[at, :], 0.0)
        for i, piece in enumerate(split(moment, pieces)):
            to = pl.ds(pl.multiple_of((leaf * pieces + i) * group, group), group)
            weight_ref[to, :] = piece.astype(bf16)
        return carry

    lax.fori_loop(0, 3 * leaves, convert, 0, unroll=8)


def near_leaves(
    first, neighbours_ref, own_ref, live, target_wide_ref,
    source_ref, weight_ref, target_ref, cube_ref, sums_ref, out_ref,
):
    count, per_leaf = live.shape
    height = 2 * group
    nbr_count = neighbours_ref.shape[1]
    deep = pieces * group
    for k in range(count):
        wide = target_wide_ref[(first + k) * height : (first + k + 1) * height, :]
        target_ref[k * per_leaf : (k + 1) * per_leaf, :] = wide.T.astype(bf16)
    for k in range(count):
        target = target_ref[k * per_leaf : (k + 1) * per_leaf, :]
        for n in range(0, nbr_count, 2):
            near = [neighbours_ref[0, n + i, first + k] for i in range(2)]
            points = [source_ref[pl.ds(pl.multiple_of(i * group, group), group), :] for i in near]
            points = jnp.concatenate(points, axis=1)
            dist_sq = jnp.dot(
                target, jnp.concatenate([points, points], axis=0), preferred_element_type=f32
            )
            inverse = lax.rsqrt(dist_sq)
            cube = (inverse * inverse * inverse).astype(bf16)
            cube_ref[k, :, n * per_leaf : (n + 2) * per_leaf] = cube
    for k in range(count):
        near = [neighbours_ref[0, n, first + k] for n in range(nbr_count)]
        weights = [weight_ref[pl.ds(pl.multiple_of(i * deep, group), deep), :] for i in near]
        total = lax.dot_general(
            cube_ref[k],
            jnp.concatenate(weights, axis=1),
            (((1,), (1,)), ((), ())),
            preferred_element_type=f32,
        ).T
        total = total[:group] + total[group : 2 * group] + total[2 * group :]
        sums_ref[pl.ds(k, group, stride=count), :] = total

    got = [sums_ref[row * count : (row + 1) * count, :] for row in range(15)]
    start, mixed, rest = got[:3], [got[3 + 3 * i : 6 + 3 * i] for i in range(3)], got[12:]
    place = [sum(split(own_ref[axis, first : first + count, :], 2)) for axis in range(3)]
    norm = dot3(place, place)
    factor = live * inv_eight_pi
    shift = dot3(place, start) - (mixed[0][0] + mixed[1][1] + mixed[2][2])
    for i in range(3):
        turned = dot3(place, [2.0 * mixed[i][j] + mixed[j][i] for j in range(3)])
        out_ref[i] = (norm * start[i] + place[i] * shift - turned + rest[i]) * factor


def far_field(sources_ref, rows_ref, tile_of, out_ref, out_hbm, pick_ref, moved_ref, out_sem):
    coeffs, slot_count = out_ref.shape[0], rows_ref.shape[0]
    directions = pick_ref.shape[0] // slot_count
    tile = moved_ref.shape[1]
    octant = rows_ref[:, coeffs : coeffs + 2].astype(f32).astype(jnp.int32)
    octant = octant[:, :1] * id_base + octant[:, 1:]
    for t in range(directions):
        hit = octant == sources_ref[0, t : t + 1, :]
        pick_ref[t * slot_count : (t + 1) * slot_count, :] = jnp.where(hit, 1.0, 0.0).astype(bf16)
    rows = rows_ref[:, :coeffs]
    stores = []
    for i, start in enumerate(range(0, coeffs, tile)):
        parts = tile_of(i)
        size = min(tile, coeffs - start)
        for t in range(directions):
            deep = parts[0].shape[1]
            moved = jnp.dot(rows[:, :deep], parts[0][t], preferred_element_type=f32)
            if deep < coeffs:
                moved += jnp.dot(rows[:, deep:], parts[1][t], preferred_element_type=f32)
            moved_ref[t * slot_count : (t + 1) * slot_count, :size] = moved.astype(bf16)
        for low in range(0, size, 2 * lanes):
            rest = min(2 * lanes, size - low)
            total = lax.dot_general(
                moved_ref[:, low : low + rest],
                pick_ref[...],
                (((0,), (0,)), ((), ())),
                preferred_element_type=f32,
            )
            at = pl.ds(start + low, rest)
            out_ref[at, :] = total.astype(bf16)
            sem = out_sem.at[len(stores)]
            stores.append(pltpu.make_async_copy(out_ref.at[at, :], out_hbm.at[at, :], sem))
            stores[-1].start()
    return stores


def near_kernel(
    slab_axis, neighbours_ref, live_ref, own_ref, odd_ref, even_ref, ops_hbm,
    early_ref, head_ref,
    point_ref, moment_ref, target_wide_ref, source_ref, weight_ref, target_ref, cube_ref, sums_ref, sem,
):
    at = (slice(None), pl.ds(0, head_ref.shape[1]), pl.ds(0, head_ref.shape[2]))
    head = pltpu.make_async_copy(ops_hbm.at[at], head_ref, sem)
    head.start()
    near_tables(
        slab_axis, own_ref, even_ref, odd_ref,
        point_ref, moment_ref, target_wide_ref, source_ref, weight_ref,
    )
    count = early_ref.shape[1]
    near_leaves(
        0, neighbours_ref, own_ref, live_ref[:count, :], target_wide_ref,
        source_ref, weight_ref, target_ref, cube_ref, sums_ref, early_ref,
    )
    early_ref[3] = live_ref[count:, :]
    head.wait()


def far_kernel(
    slab_axis, neighbours_ref, own_ref, odd_ref, even_ref, picks_ref, rows_ref, head_ref, early_ref,
    ops_hbm, local_hbm, velocity_hbm,
    point_ref, moment_ref, target_wide_ref, source_ref, weight_ref, target_ref, cube_ref, sums_ref,
    ops_ref, pick_ref, moved_ref, local_ref, late_ref, velocity_ref, ops_sem, out_sem,
):
    coeffs, tile = ops_hbm.shape[1], moved_ref.shape[1]
    deep = head_ref.shape[1]
    rest = (slice(None), pl.ds(deep, coeffs - deep), pl.ds(0, tile))
    loads = [pltpu.make_async_copy(ops_hbm.at[rest], ops_ref.at[rest], ops_sem.at[0])]
    loads[0].start()
    for i, start in enumerate(range(tile, coeffs, tile)):
        at = pl.ds(start, min(tile, coeffs - start))
        loads.append(pltpu.make_async_copy(ops_hbm.at[:, :, at], ops_ref.at[:, :, at], ops_sem.at[i + 1]))
        loads[-1].start()

    count = early_ref.shape[1]
    near_tables(
        slab_axis, own_ref, even_ref, odd_ref,
        point_ref, moment_ref, target_wide_ref, source_ref, weight_ref,
    )
    near_leaves(
        count, neighbours_ref, own_ref, early_ref[3], target_wide_ref,
        source_ref, weight_ref, target_ref, cube_ref, sums_ref, late_ref,
    )
    for axis in range(3):
        velocity_ref[axis, :count, :] = early_ref[axis]
        velocity_ref[axis, count:, :] = late_ref[axis]
    velocity_store = pltpu.make_async_copy(velocity_ref, velocity_hbm, ops_sem.at[len(loads)])
    velocity_store.start()

    def tile_of(i):
        loads[i].wait()
        if i == 0:
            return (head_ref, ops_ref.at[rest])
        return (ops_ref.at[:, :, pl.ds(i * tile, min(tile, coeffs - i * tile))],)

    stores = far_field(picks_ref, rows_ref, tile_of, local_ref, local_hbm, pick_ref, moved_ref, out_sem)
    for store in stores + [velocity_store]:
        store.wait()


def vmem():
    return pl.BlockSpec(memory_space=pltpu.VMEM)


def in_hbm(array):
    return pltpu.with_memory_space_constraint(array, pltpu.HBM)


def smem():
    return pl.BlockSpec(memory_space=pltpu.SMEM)


def hbm():
    return pl.BlockSpec(memory_space=pltpu.HBM)


def near_scratch(neighbours, packed):
    _, leaves, per_leaf = packed.shape
    table, count = 3 * leaves, leaves // 2
    return [
        pltpu.VMEM((table * group, per_leaf), f32),
        pltpu.VMEM((table * group, per_leaf), f32),
        pltpu.VMEM((leaves * 2 * group, per_leaf), f32),
        pltpu.VMEM((table * group, per_leaf), bf16),
        pltpu.VMEM((table * pieces * group, per_leaf), bf16),
        pltpu.VMEM((count * per_leaf, 2 * group), bf16),
        pltpu.VMEM((count, per_leaf, neighbours.shape[1] * per_leaf), bf16),
        pltpu.VMEM((group * count, per_leaf), f32),
    ]


def call_near(neighbours, live, packed, odd, even, m2l_ops, tile):
    _, leaves, per_leaf = packed.shape
    directions, coeffs, _ = m2l_ops.shape
    return pl.pallas_call(
        functools.partial(near_kernel, "nb"),
        out_shape=(
            pltpu.VMEM((4, leaves // 2, per_leaf), f32),
            pltpu.VMEM((directions, coeffs // lanes * lanes, tile), bf16),
        ),
        in_specs=[smem()] + [vmem()] * 4 + [hbm()],
        out_specs=(vmem(), vmem()),
        scratch_shapes=near_scratch(neighbours, packed) + [pltpu.SemaphoreType.DMA],
        compiler_params=pltpu.CompilerParams(vmem_limit_bytes=24 * 2**20),
        name="near",
    )(neighbours, live, packed, odd, even, in_hbm(m2l_ops))


def call_far(neighbours, packed, odd, even, m2l_sources, arrived, head, early, m2l_ops):
    _, leaves, per_leaf = packed.shape
    directions, coeffs, _ = m2l_ops.shape
    tile = head.shape[2]
    owned = m2l_sources.shape[2]
    picks = directions * arrived.shape[0]
    steps = -(-coeffs // tile)
    return pl.pallas_call(
        functools.partial(far_kernel, "nb"),
        out_shape=(
            jax.ShapeDtypeStruct((coeffs, owned), bf16),
            jax.ShapeDtypeStruct((3, leaves, per_leaf), f32),
        ),
        in_specs=[smem()] + [vmem()] * 7 + [hbm()],
        out_specs=(hbm(), hbm()),
        scratch_shapes=near_scratch(neighbours, packed)
        + [
            pltpu.VMEM(m2l_ops.shape, bf16),
            pltpu.VMEM((picks, owned), bf16),
            pltpu.VMEM((picks, tile), bf16),
            pltpu.VMEM((coeffs, owned), bf16),
            pltpu.VMEM((3, leaves - leaves // 2, per_leaf), f32),
            pltpu.VMEM((3, leaves, per_leaf), f32),
            pltpu.SemaphoreType.DMA((steps + 1,)),
            pltpu.SemaphoreType.DMA((2 * steps,)),
        ],
        compiler_params=pltpu.CompilerParams(vmem_limit_bytes=40 * 2**20),
        name="far",
    )(neighbours, packed, odd, even, m2l_sources, arrived, head, early, in_hbm(m2l_ops))


def call_presum(hx_count, partial_multipoles, shared_slots, positions, forces, leaf_counts, neighbours):
    row_count, coeffs = partial_multipoles.shape[1:]
    cap = row_count // hx_count
    uniq = cap // 4
    slot_count = hx_count * uniq
    width = -(-(coeffs + 2) // lanes) * lanes
    tile = width
    steps = -(-coeffs // tile)
    leaves = leaf_counts.shape[1]
    per_leaf = positions.shape[2] // leaves

    return pl.pallas_call(
        functools.partial(presum_kernel, cap, uniq, tile),
        out_shape=(
            jax.ShapeDtypeStruct((slot_count, width), bf16),
            pltpu.VMEM((6, leaves, per_leaf), f32),
            pltpu.VMEM((9, leaves, per_leaf), bf16),
            pltpu.VMEM((leaves, per_leaf), f32),
            pltpu.SMEM(neighbours.shape, jnp.int32),
        ),
        in_specs=[hbm()] * 6,
        out_specs=(hbm(), vmem(), vmem(), vmem(), smem()),
        scratch_shapes=[
            pltpu.VMEM(leaf_counts.shape, jnp.int32),
            pltpu.VMEM(shared_slots.shape, jnp.int32),
            pltpu.VMEM((coeffs, row_count), bf16),
            pltpu.VMEM((3, leaves, per_leaf), f32),
            pltpu.VMEM((3, leaves, per_leaf), f32),
            pltpu.VMEM((slot_count, width), bf16),
            pltpu.SemaphoreType.DMA((5,)),
            pltpu.SemaphoreType.DMA((steps,)),
            pltpu.SemaphoreType.DMA((steps,)),
        ],
        compiler_params=pltpu.CompilerParams(vmem_limit_bytes=16 * 2**20),
        name="presum",
    )(
        *map(
            in_hbm,
            (
                leaf_counts,
                shared_slots,
                partial_multipoles[0].T,
                positions[0].reshape(3, leaves, per_leaf),
                forces[0].reshape(3, leaves, per_leaf),
                neighbours,
            ),
        )
    )


def on_device(
    partial_multipoles,
    shared_slots,
    m2l_sources,
    m2l_ops,
    positions,
    forces,
    leaf_counts,
    neighbours,
):
    hx_count, nb_count = lax.axis_size("hx"), lax.axis_size("nb")
    sums, packed, sent, live, sources = call_presum(
        hx_count, partial_multipoles, shared_slots, positions, forces, leaf_counts, neighbours
    )

    even_pairs = [(i, i + 1) for i in range(0, nb_count - 1, 2)]
    odd_pairs = [(i, i + 1) for i in range(1, nb_count - 1, 2)]
    even = lax.ppermute(sent, "nb", even_pairs + [(j, i) for i, j in even_pairs])
    odd = lax.ppermute(sent, "nb", odd_pairs + [(j, i) for i, j in odd_pairs])
    arrived = lax.all_to_all(
        sums.reshape(hx_count, -1, sums.shape[1]), "hx", split_axis=0, concat_axis=0, tiled=True
    ).reshape(sums.shape)

    early, head = call_near(sources, live, packed, odd, even, m2l_ops, 4 * lanes)
    local, velocity = call_far(
        sources, packed, odd, even, m2l_sources, arrived, head, early, m2l_ops
    )

    return local.T[None], velocity.reshape(positions.shape)


def solution(mesh):
    placed = (
        P("nb", "hx", None),
        P("nb", "hx"),
        P("nb", None, "hx"),
        P(),
        P("nb", None, "hx"),
        P("nb", None, "hx"),
        P("nb", "hx"),
        P("nb", None, "hx"),
    )
    return jax.shard_map(
        on_device,
        mesh=mesh,
        in_specs=placed,
        out_specs=(P("nb", "hx", None), P("nb", None, "hx")),
        check_vma=False,
    )
```

```python
import functools
import math

import jax
import jax.numpy as jnp
from jax import lax
from jax.experimental import pallas as pl
from jax.experimental.pallas import tpu as pltpu
from jax.sharding import PartitionSpec as P

reg_eps2 = 0.01
inv_eight_pi = 1.0 / (8.0 * math.pi)
id_base = 32
lanes = 128
group = 16
pieces = 3
bf16 = jnp.bfloat16
f32 = jnp.float32


def split(value, count):
    pieces = []
    for _ in range(count):
        piece = value.astype(bf16).astype(f32)
        pieces.append(piece)
        value = value - piece
    return pieces


def presum_kernel(
    cap, uniq, tile, counts_hbm, slots_hbm, rows_hbm, pos_hbm, frc_hbm, neighbours_hbm,
    sums_hbm, packed_ref, sent_ref, live_ref, neighbours_out,
    counts_ref, slots_ref, rows_ref, pos_ref, frc_ref, sums_ref, arrival, rows_sem, sums_sem,
):
    coeffs, row_count = rows_ref.shape
    slot_count, width = sums_ref.shape
    spans = [(start, min(tile, coeffs - start)) for start in range(0, coeffs, tile)]
    pairs = (
        (slots_hbm, slots_ref),
        (counts_hbm, counts_ref),
        (pos_hbm, pos_ref),
        (frc_hbm, frc_ref),
        (neighbours_hbm, neighbours_out),
    )
    copies = [pltpu.make_async_copy(a, b, arrival.at[i]) for i, (a, b) in enumerate(pairs)]
    loads = []
    for i, (start, size) in enumerate(spans):
        at = pl.ds(start, size)
        loads.append(pltpu.make_async_copy(rows_hbm.at[at, :], rows_ref.at[at, :], rows_sem.at[i]))
    for copy in copies[:1] + loads + copies[1:]:
        copy.start()
    copies[0].wait()

    targets = []
    sub_at = lax.broadcasted_iota(jnp.int32, (lanes, lanes), 0)
    lane_at = lax.broadcasted_iota(jnp.int32, (lanes, lanes), 1)
    same_block = (sub_at // cap) == (lane_at // cap)
    for start in range(0, row_count, lanes):
        by_lane = jnp.broadcast_to(slots_ref[:, start : start + lanes], (lanes, lanes))
        by_sub = by_lane.T
        equal = same_block & (by_lane == by_sub)
        seen = jnp.where(equal & (lane_at < sub_at), 1, 0)
        first = (jnp.max(seen, axis=1, keepdims=True) == 0) & (by_sub >= 0)
        below = jnp.where(first & same_block & (by_sub < by_lane), 1, 0)
        rank = jnp.sum(below, axis=0, keepdims=True)
        lane_row = lax.broadcasted_iota(jnp.int32, (1, lanes), 1) + start
        block = lane_row // cap
        valid = slots_ref[:, start : start + lanes] >= 0
        targets.append(jnp.where(valid, block * uniq + rank, -1))
    target = jnp.concatenate(targets, axis=1)
    slot_at = lax.broadcasted_iota(jnp.int32, (slot_count, row_count), 0)
    hit = slot_at == target
    octant = jnp.max(jnp.where(hit, slots_ref[...], -1), axis=1, keepdims=True)
    one_hot = jnp.where(hit, 1.0, 0.0).astype(bf16)
    high = octant // id_base
    low = octant - high * id_base
    extra_at = lax.broadcasted_iota(jnp.int32, (slot_count, width - coeffs), 1)
    extra = jnp.where(extra_at == 0, high, jnp.where(extra_at == 1, low, 0))
    sums_ref[:, coeffs:] = extra.astype(f32).astype(bf16)
    stores = []
    for i, (start, size) in enumerate(spans):
        loads[i].wait()
        sums = lax.dot_general(
            one_hot,
            rows_ref[start : start + size, :],
            (((1,), (1,)), ((), ())),
            preferred_element_type=f32,
        )
        sums_ref[:, start : start + size] = sums.astype(bf16)
        at = pl.ds(start, min(tile, width - start))
        stores.append(pltpu.make_async_copy(sums_ref.at[:, at], sums_hbm.at[:, at], sums_sem.at[i]))
        stores[-1].start()
    for copy in copies[1:]:
        copy.wait()
    leaves, per_leaf = pos_ref.shape[1:]
    blank = jnp.zeros((1, lanes - leaves), jnp.int32)
    count = jnp.concatenate([counts_ref[...], blank], axis=1)
    count = jnp.broadcast_to(count, (lanes, lanes)).T[:leaves]
    point_at = lax.broadcasted_iota(jnp.int32, (leaves, per_leaf), 1)
    live = jnp.where(point_at < count, 1.0, 0.0)
    live_ref[...] = live
    for axis in range(3):
        masked = frc_ref[axis] * live
        packed_ref[axis] = pos_ref[axis]
        packed_ref[3 + axis] = masked
        high, low = split(pos_ref[axis], 2)
        for row, value in enumerate((high, low, masked)):
            sent_ref[3 * row + axis] = value.astype(bf16)
    for store in stores:
        store.wait()


def dot3(left, right):
    return left[0] * right[0] + left[1] * right[1] + left[2] * right[2]


def near_tables(
    slab_axis, own_ref, even_ref, odd_ref, point_ref, moment_ref, target_wide_ref, source_ref, weight_ref
):
    _, leaves, per_leaf = own_ref.shape
    even = lax.rem(lax.axis_index(slab_axis), 2) == 0

    def stored(ref, leaf_start, height, rows):
        for row, value in enumerate(rows):
            ref[pl.ds(leaf_start * height + row, leaves, stride=height), :] = value

    for part in range(3):
        if part == 1:
            cut = [split(own_ref[c], 2) for c in range(3)]
            force = [own_ref[3 + c] for c in range(3)]
        else:
            refs = (odd_ref, even_ref) if part == 0 else (even_ref, odd_ref)
            comp = [jnp.where(even, refs[0][c], refs[1][c]).astype(f32) for c in range(9)]
            cut = [comp[c : c + 4 : 3] for c in range(3)]
            force = comp[6:]
        place = [high + low for high, low in cut]
        norm = dot3(place, place)
        along = dot3(force, place)
        size = split(norm + reg_eps2, 3)
        stored(point_ref, part * leaves, group, [c[0] for c in cut] + [c[1] for c in cut] + size)
        moments = force + [force[i] * place[j] for i in range(3) for j in range(3)]
        moments += [force[i] * (norm + 2.0 * reg_eps2) + along * place[i] for i in range(3)]
        stored(moment_ref, part * leaves, group, moments)
        if part == 1:
            zero, one = jnp.zeros_like(norm), jnp.ones_like(norm)
            high = [-2.0 * c[0] for c in cut]
            low = [-2.0 * c[1] for c in cut]
            rows = high + high + [one] * 3 + split(norm, 3) + [zero] * 4 + low + low + [zero] * 10
            stored(target_wide_ref, 0, 2 * group, rows)

    row_at = lax.broadcasted_iota(jnp.int32, (group, per_leaf), 0)

    def convert(leaf, carry):
        at = pl.ds(pl.multiple_of(leaf * group, group), group)
        point = jnp.where(row_at < 9, point_ref[at, :], jnp.where(row_at < 12, 1.0, 0.0))
        source_ref[at, :] = point.astype(bf16)
        moment = jnp.where(row_at < 15, moment_ref[at, :], 0.0)
        for i, piece in enumerate(split(moment, pieces)):
            to = pl.ds(pl.multiple_of((leaf * pieces + i) * group, group), group)
            weight_ref[to, :] = piece.astype(bf16)
        return carry

    lax.fori_loop(0, 3 * leaves, convert, 0, unroll=8)


def near_leaves(
    first, neighbours_ref, own_ref, live, target_wide_ref,
    source_ref, weight_ref, target_ref, cube_ref, sums_ref, out_ref,
):
    count, per_leaf = live.shape
    height = 2 * group
    nbr_count = neighbours_ref.shape[1]
    deep = pieces * group
    for k in range(count):
        wide = target_wide_ref[(first + k) * height : (first + k + 1) * height, :]
        target_ref[k * per_leaf : (k + 1) * per_leaf, :] = wide.T.astype(bf16)
    for k in range(count):
        target = target_ref[k * per_leaf : (k + 1) * per_leaf, :]
        for n in range(0, nbr_count, 2):
            near = [neighbours_ref[0, n + i, first + k] for i in range(2)]
            points = [source_ref[pl.ds(pl.multiple_of(i * group, group), group), :] for i in near]
            points = jnp.concatenate(points, axis=1)
            dist_sq = jnp.dot(
                target, jnp.concatenate([points, points], axis=0), preferred_element_type=f32
            )
            inverse = lax.rsqrt(dist_sq)
            cube = (inverse * inverse * inverse).astype(bf16)
            cube_ref[k, :, n * per_leaf : (n + 2) * per_leaf] = cube
    for k in range(count):
        near = [neighbours_ref[0, n, first + k] for n in range(nbr_count)]
        weights = [weight_ref[pl.ds(pl.multiple_of(i * deep, group), deep), :] for i in near]
        total = lax.dot_general(
            cube_ref[k],
            jnp.concatenate(weights, axis=1),
            (((1,), (1,)), ((), ())),
            preferred_element_type=f32,
        ).T
        total = total[:group] + total[group : 2 * group] + total[2 * group :]
        sums_ref[pl.ds(k, group, stride=count), :] = total

    got = [sums_ref[row * count : (row + 1) * count, :] for row in range(15)]
    start, mixed, rest = got[:3], [got[3 + 3 * i : 6 + 3 * i] for i in range(3)], got[12:]
    place = [sum(split(own_ref[axis, first : first + count, :], 2)) for axis in range(3)]
    norm = dot3(place, place)
    factor = live * inv_eight_pi
    shift = dot3(place, start) - (mixed[0][0] + mixed[1][1] + mixed[2][2])
    for i in range(3):
        turned = dot3(place, [2.0 * mixed[i][j] + mixed[j][i] for j in range(3)])
        out_ref[i] = (norm * start[i] + place[i] * shift - turned + rest[i]) * factor


def far_field(sources_ref, rows_ref, tile_of, out_ref, out_hbm, pick_ref, moved_ref, out_sem):
    coeffs, slot_count = out_ref.shape[0], rows_ref.shape[0]
    directions = pick_ref.shape[0] // slot_count
    tile = moved_ref.shape[1]
    octant = rows_ref[:, coeffs : coeffs + 2].astype(f32).astype(jnp.int32)
    octant = octant[:, :1] * id_base + octant[:, 1:]
    for t in range(directions):
        hit = octant == sources_ref[0, t : t + 1, :]
        pick_ref[t * slot_count : (t + 1) * slot_count, :] = jnp.where(hit, 1.0, 0.0).astype(bf16)
    rows = rows_ref[:, :coeffs]
    stores = []
    for i, start in enumerate(range(0, coeffs, tile)):
        ops_ref = tile_of(i)
        size = min(tile, coeffs - start)
        for t in range(directions):
            moved = jnp.dot(rows, ops_ref[t], preferred_element_type=f32)
            moved_ref[t * slot_count : (t + 1) * slot_count, :size] = moved.astype(bf16)
        for low in range(0, size, 2 * lanes):
            rest = min(2 * lanes, size - low)
            total = lax.dot_general(
                moved_ref[:, low : low + rest],
                pick_ref[...],
                (((0,), (0,)), ((), ())),
                preferred_element_type=f32,
            )
            at = pl.ds(start + low, rest)
            out_ref[at, :] = total.astype(bf16)
            sem = out_sem.at[len(stores)]
            stores.append(pltpu.make_async_copy(out_ref.at[at, :], out_hbm.at[at, :], sem))
            stores[-1].start()
    return stores


def near_kernel(
    slab_axis, neighbours_ref, live_ref, own_ref, odd_ref, even_ref, ops_hbm,
    early_ref, head_ref,
    point_ref, moment_ref, target_wide_ref, source_ref, weight_ref, target_ref, cube_ref, sums_ref, sem,
):
    at = (slice(None), pl.ds(0, head_ref.shape[1]), pl.ds(0, head_ref.shape[2]))
    head = pltpu.make_async_copy(ops_hbm.at[at], head_ref, sem)
    head.start()
    near_tables(
        slab_axis, own_ref, even_ref, odd_ref,
        point_ref, moment_ref, target_wide_ref, source_ref, weight_ref,
    )
    count = early_ref.shape[1]
    near_leaves(
        0, neighbours_ref, own_ref, live_ref[:count, :], target_wide_ref,
        source_ref, weight_ref, target_ref, cube_ref, sums_ref, early_ref,
    )
    early_ref[3] = live_ref[count:, :]
    head.wait()


def far_kernel(
    slab_axis, neighbours_ref, own_ref, odd_ref, even_ref, picks_ref, rows_ref, head_ref, early_ref,
    ops_hbm, local_hbm, velocity_hbm,
    point_ref, moment_ref, target_wide_ref, source_ref, weight_ref, target_ref, cube_ref, sums_ref,
    ops_ref, pick_ref, moved_ref, local_ref, late_ref, velocity_ref, ops_sem, out_sem,
):
    coeffs, tile = ops_hbm.shape[1], moved_ref.shape[1]
    loads = [None]
    for i, start in enumerate(range(tile, coeffs, tile)):
        at = pl.ds(start, min(tile, coeffs - start))
        loads.append(pltpu.make_async_copy(ops_hbm.at[:, :, at], ops_ref.at[:, :, at], ops_sem.at[i + 1]))
        loads[-1].start()

    count = early_ref.shape[1]
    near_tables(
        slab_axis, own_ref, even_ref, odd_ref,
        point_ref, moment_ref, target_wide_ref, source_ref, weight_ref,
    )
    near_leaves(
        count, neighbours_ref, own_ref, early_ref[3], target_wide_ref,
        source_ref, weight_ref, target_ref, cube_ref, sums_ref, late_ref,
    )
    for axis in range(3):
        velocity_ref[axis, :count, :] = early_ref[axis]
        velocity_ref[axis, count:, :] = late_ref[axis]
    velocity_store = pltpu.make_async_copy(velocity_ref, velocity_hbm, ops_sem.at[len(loads)])
    velocity_store.start()

    def tile_of(i):
        if i == 0:
            return head_ref
        loads[i].wait()
        return ops_ref.at[:, :, pl.ds(i * tile, min(tile, coeffs - i * tile))]

    stores = far_field(picks_ref, rows_ref, tile_of, local_ref, local_hbm, pick_ref, moved_ref, out_sem)
    for store in stores + [velocity_store]:
        store.wait()


def vmem():
    return pl.BlockSpec(memory_space=pltpu.VMEM)


def in_hbm(array):
    return pltpu.with_memory_space_constraint(array, pltpu.HBM)


def smem():
    return pl.BlockSpec(memory_space=pltpu.SMEM)


def hbm():
    return pl.BlockSpec(memory_space=pltpu.HBM)


def near_scratch(neighbours, packed):
    _, leaves, per_leaf = packed.shape
    table, count = 3 * leaves, leaves // 2
    return [
        pltpu.VMEM((table * group, per_leaf), f32),
        pltpu.VMEM((table * group, per_leaf), f32),
        pltpu.VMEM((leaves * 2 * group, per_leaf), f32),
        pltpu.VMEM((table * group, per_leaf), bf16),
        pltpu.VMEM((table * pieces * group, per_leaf), bf16),
        pltpu.VMEM((count * per_leaf, 2 * group), bf16),
        pltpu.VMEM((count, per_leaf, neighbours.shape[1] * per_leaf), bf16),
        pltpu.VMEM((group * count, per_leaf), f32),
    ]


def call_near(neighbours, live, packed, odd, even, m2l_ops, tile):
    _, leaves, per_leaf = packed.shape
    directions, coeffs, _ = m2l_ops.shape
    return pl.pallas_call(
        functools.partial(near_kernel, "nb"),
        out_shape=(
            pltpu.VMEM((4, leaves // 2, per_leaf), f32),
            pltpu.VMEM((directions, coeffs, tile), bf16),
        ),
        in_specs=[smem()] + [vmem()] * 4 + [hbm()],
        out_specs=(vmem(), vmem()),
        scratch_shapes=near_scratch(neighbours, packed) + [pltpu.SemaphoreType.DMA],
        compiler_params=pltpu.CompilerParams(vmem_limit_bytes=24 * 2**20),
        name="near",
    )(neighbours, live, packed, odd, even, in_hbm(m2l_ops))


def call_far(neighbours, packed, odd, even, m2l_sources, arrived, head, early, m2l_ops):
    _, leaves, per_leaf = packed.shape
    directions, coeffs, _ = m2l_ops.shape
    tile = head.shape[2]
    owned = m2l_sources.shape[2]
    picks = directions * arrived.shape[0]
    steps = -(-coeffs // tile)
    return pl.pallas_call(
        functools.partial(far_kernel, "nb"),
        out_shape=(
            jax.ShapeDtypeStruct((coeffs, owned), bf16),
            jax.ShapeDtypeStruct((3, leaves, per_leaf), f32),
        ),
        in_specs=[smem()] + [vmem()] * 7 + [hbm()],
        out_specs=(hbm(), hbm()),
        scratch_shapes=near_scratch(neighbours, packed)
        + [
            pltpu.VMEM(m2l_ops.shape, bf16),
            pltpu.VMEM((picks, owned), bf16),
            pltpu.VMEM((picks, tile), bf16),
            pltpu.VMEM((coeffs, owned), bf16),
            pltpu.VMEM((3, leaves - leaves // 2, per_leaf), f32),
            pltpu.VMEM((3, leaves, per_leaf), f32),
            pltpu.SemaphoreType.DMA((steps + 1,)),
            pltpu.SemaphoreType.DMA((2 * steps,)),
        ],
        compiler_params=pltpu.CompilerParams(vmem_limit_bytes=40 * 2**20),
        name="far",
    )(neighbours, packed, odd, even, m2l_sources, arrived, head, early, in_hbm(m2l_ops))


def call_presum(hx_count, partial_multipoles, shared_slots, positions, forces, leaf_counts, neighbours):
    row_count, coeffs = partial_multipoles.shape[1:]
    cap = row_count // hx_count
    uniq = cap // 4
    slot_count = hx_count * uniq
    width = -(-(coeffs + 2) // lanes) * lanes
    tile = width
    steps = -(-coeffs // tile)
    leaves = leaf_counts.shape[1]
    per_leaf = positions.shape[2] // leaves

    return pl.pallas_call(
        functools.partial(presum_kernel, cap, uniq, tile),
        out_shape=(
            jax.ShapeDtypeStruct((slot_count, width), bf16),
            pltpu.VMEM((6, leaves, per_leaf), f32),
            pltpu.VMEM((9, leaves, per_leaf), bf16),
            pltpu.VMEM((leaves, per_leaf), f32),
            pltpu.SMEM(neighbours.shape, jnp.int32),
        ),
        in_specs=[hbm()] * 6,
        out_specs=(hbm(), vmem(), vmem(), vmem(), smem()),
        scratch_shapes=[
            pltpu.VMEM(leaf_counts.shape, jnp.int32),
            pltpu.VMEM(shared_slots.shape, jnp.int32),
            pltpu.VMEM((coeffs, row_count), bf16),
            pltpu.VMEM((3, leaves, per_leaf), f32),
            pltpu.VMEM((3, leaves, per_leaf), f32),
            pltpu.VMEM((slot_count, width), bf16),
            pltpu.SemaphoreType.DMA((5,)),
            pltpu.SemaphoreType.DMA((steps,)),
            pltpu.SemaphoreType.DMA((steps,)),
        ],
        compiler_params=pltpu.CompilerParams(vmem_limit_bytes=16 * 2**20),
        name="presum",
    )(
        *map(
            in_hbm,
            (
                leaf_counts,
                shared_slots,
                partial_multipoles[0].T,
                positions[0].reshape(3, leaves, per_leaf),
                forces[0].reshape(3, leaves, per_leaf),
                neighbours,
            ),
        )
    )


def on_device(
    partial_multipoles,
    shared_slots,
    m2l_sources,
    m2l_ops,
    positions,
    forces,
    leaf_counts,
    neighbours,
):
    hx_count, nb_count = lax.axis_size("hx"), lax.axis_size("nb")
    sums, packed, sent, live, sources = call_presum(
        hx_count, partial_multipoles, shared_slots, positions, forces, leaf_counts, neighbours
    )

    even_pairs = [(i, i + 1) for i in range(0, nb_count - 1, 2)]
    odd_pairs = [(i, i + 1) for i in range(1, nb_count - 1, 2)]
    even = lax.ppermute(sent, "nb", even_pairs + [(j, i) for i, j in even_pairs])
    odd = lax.ppermute(sent, "nb", odd_pairs + [(j, i) for i, j in odd_pairs])
    arrived = lax.all_to_all(
        sums.reshape(hx_count, -1, sums.shape[1]), "hx", split_axis=0, concat_axis=0, tiled=True
    ).reshape(sums.shape)

    early, head = call_near(sources, live, packed, odd, even, m2l_ops, 4 * lanes)
    local, velocity = call_far(
        sources, packed, odd, even, m2l_sources, arrived, head, early, m2l_ops
    )

    return local.T[None], velocity.reshape(positions.shape)


def solution(mesh):
    placed = (
        P("nb", "hx", None),
        P("nb", "hx"),
        P("nb", None, "hx"),
        P(),
        P("nb", None, "hx"),
        P("nb", None, "hx"),
        P("nb", "hx"),
        P("nb", None, "hx"),
    )
    return jax.shard_map(
        on_device,
        mesh=mesh,
        in_specs=placed,
        out_specs=(P("nb", "hx", None), P("nb", None, "hx")),
        check_vma=False,
    )
```

```python
import functools
import math

import jax
import jax.numpy as jnp
from jax import lax
from jax.experimental import pallas as pl
from jax.experimental.pallas import tpu as pltpu
from jax.sharding import PartitionSpec as P

reg_eps2 = 0.01
inv_eight_pi = 1.0 / (8.0 * math.pi)
id_base = 32
lanes = 128
group = 16
pieces = 2
bf16 = jnp.bfloat16
f32 = jnp.float32


def split(value, count):
    pieces = []
    for _ in range(count):
        piece = value.astype(bf16).astype(f32)
        pieces.append(piece)
        value = value - piece
    return pieces


def presum_kernel(
    cap, uniq, tile, counts_hbm, slots_hbm, rows_hbm, pos_hbm, frc_hbm, neighbours_hbm,
    sums_hbm, packed_ref, sent_ref, live_ref, neighbours_out,
    counts_ref, slots_ref, rows_ref, pos_ref, frc_ref, sums_ref, arrival, rows_sem, sums_sem,
):
    coeffs, row_count = rows_ref.shape
    slot_count, width = sums_ref.shape
    spans = [(start, min(tile, coeffs - start)) for start in range(0, coeffs, tile)]
    pairs = (
        (slots_hbm, slots_ref),
        (counts_hbm, counts_ref),
        (pos_hbm, pos_ref),
        (frc_hbm, frc_ref),
        (neighbours_hbm, neighbours_out),
    )
    copies = [pltpu.make_async_copy(a, b, arrival.at[i]) for i, (a, b) in enumerate(pairs)]
    loads = []
    for i, (start, size) in enumerate(spans):
        at = pl.ds(start, size)
        loads.append(pltpu.make_async_copy(rows_hbm.at[at, :], rows_ref.at[at, :], rows_sem.at[i]))
    for copy in copies[:1] + loads + copies[1:]:
        copy.start()
    copies[0].wait()

    targets = []
    sub_at = lax.broadcasted_iota(jnp.int32, (lanes, lanes), 0)
    lane_at = lax.broadcasted_iota(jnp.int32, (lanes, lanes), 1)
    same_block = (sub_at // cap) == (lane_at // cap)
    for start in range(0, row_count, lanes):
        by_lane = jnp.broadcast_to(slots_ref[:, start : start + lanes], (lanes, lanes))
        by_sub = by_lane.T
        equal = same_block & (by_lane == by_sub)
        seen = jnp.where(equal & (lane_at < sub_at), 1, 0)
        first = (jnp.max(seen, axis=1, keepdims=True) == 0) & (by_sub >= 0)
        below = jnp.where(first & same_block & (by_sub < by_lane), 1, 0)
        rank = jnp.sum(below, axis=0, keepdims=True)
        lane_row = lax.broadcasted_iota(jnp.int32, (1, lanes), 1) + start
        block = lane_row // cap
        valid = slots_ref[:, start : start + lanes] >= 0
        targets.append(jnp.where(valid, block * uniq + rank, -1))
    target = jnp.concatenate(targets, axis=1)
    slot_at = lax.broadcasted_iota(jnp.int32, (slot_count, row_count), 0)
    hit = slot_at == target
    octant = jnp.max(jnp.where(hit, slots_ref[...], -1), axis=1, keepdims=True)
    one_hot = jnp.where(hit, 1.0, 0.0).astype(bf16)
    high = octant // id_base
    low = octant - high * id_base
    extra_at = lax.broadcasted_iota(jnp.int32, (slot_count, width - coeffs), 1)
    extra = jnp.where(extra_at == 0, high, jnp.where(extra_at == 1, low, 0))
    sums_ref[:, coeffs:] = extra.astype(f32).astype(bf16)
    stores = []
    for i, (start, size) in enumerate(spans):
        loads[i].wait()
        sums = lax.dot_general(
            one_hot,
            rows_ref[start : start + size, :],
            (((1,), (1,)), ((), ())),
            preferred_element_type=f32,
        )
        sums_ref[:, start : start + size] = sums.astype(bf16)
        at = pl.ds(start, min(tile, width - start))
        stores.append(pltpu.make_async_copy(sums_ref.at[:, at], sums_hbm.at[:, at], sums_sem.at[i]))
        stores[-1].start()
    for copy in copies[1:]:
        copy.wait()
    leaves, per_leaf = pos_ref.shape[1:]
    blank = jnp.zeros((1, lanes - leaves), jnp.int32)
    count = jnp.concatenate([counts_ref[...], blank], axis=1)
    count = jnp.broadcast_to(count, (lanes, lanes)).T[:leaves]
    point_at = lax.broadcasted_iota(jnp.int32, (leaves, per_leaf), 1)
    live = jnp.where(point_at < count, 1.0, 0.0)
    live_ref[...] = live
    for axis in range(3):
        masked = frc_ref[axis] * live
        packed_ref[axis] = pos_ref[axis]
        packed_ref[3 + axis] = masked
        high, low = split(pos_ref[axis], 2)
        for row, value in enumerate((high, low, masked)):
            sent_ref[3 * row + axis] = value.astype(bf16)
    for store in stores:
        store.wait()


def dot3(left, right):
    return left[0] * right[0] + left[1] * right[1] + left[2] * right[2]


def near_tables(
    slab_axis, own_ref, even_ref, odd_ref, point_ref, moment_ref, target_wide_ref, source_ref, weight_ref
):
    _, leaves, per_leaf = own_ref.shape
    even = lax.rem(lax.axis_index(slab_axis), 2) == 0

    def stored(ref, leaf_start, height, rows):
        for row, value in enumerate(rows):
            ref[pl.ds(leaf_start * height + row, leaves, stride=height), :] = value

    for part in range(3):
        if part == 1:
            cut = [split(own_ref[c], 2) for c in range(3)]
            force = [own_ref[3 + c] for c in range(3)]
        else:
            refs = (odd_ref, even_ref) if part == 0 else (even_ref, odd_ref)
            comp = [jnp.where(even, refs[0][c], refs[1][c]).astype(f32) for c in range(9)]
            cut = [comp[c : c + 4 : 3] for c in range(3)]
            force = comp[6:]
        place = [high + low for high, low in cut]
        norm = dot3(place, place)
        along = dot3(force, place)
        size = split(norm + reg_eps2, 3)
        stored(point_ref, part * leaves, group, [c[0] for c in cut] + [c[1] for c in cut] + size)
        moments = force + [force[i] * place[j] for i in range(3) for j in range(3)]
        moments += [force[i] * (norm + 2.0 * reg_eps2) + along * place[i] for i in range(3)]
        stored(moment_ref, part * leaves, group, moments)
        if part == 1:
            zero, one = jnp.zeros_like(norm), jnp.ones_like(norm)
            high = [-2.0 * c[0] for c in cut]
            low = [-2.0 * c[1] for c in cut]
            rows = high + high + [one] * 3 + split(norm, 3) + [zero] * 4 + low + low + [zero] * 10
            stored(target_wide_ref, 0, 2 * group, rows)

    row_at = lax.broadcasted_iota(jnp.int32, (group, per_leaf), 0)

    def convert(leaf, carry):
        at = pl.ds(pl.multiple_of(leaf * group, group), group)
        point = jnp.where(row_at < 9, point_ref[at, :], jnp.where(row_at < 12, 1.0, 0.0))
        source_ref[at, :] = point.astype(bf16)
        moment = jnp.where(row_at < 15, moment_ref[at, :], 0.0)
        for i, piece in enumerate(split(moment, pieces)):
            to = pl.ds(pl.multiple_of((leaf * pieces + i) * group, group), group)
            weight_ref[to, :] = piece.astype(bf16)
        return carry

    lax.fori_loop(0, 3 * leaves, convert, 0, unroll=8)


def near_leaves(
    first, neighbours_ref, own_ref, live, target_wide_ref,
    source_ref, weight_ref, target_ref, cube_ref, sums_ref, out_ref,
):
    count, per_leaf = live.shape
    height = 2 * group
    nbr_count = neighbours_ref.shape[1]
    deep = pieces * group
    for k in range(count):
        wide = target_wide_ref[(first + k) * height : (first + k + 1) * height, :]
        target_ref[k * per_leaf : (k + 1) * per_leaf, :] = wide.T.astype(bf16)
    for k in range(count):
        target = target_ref[k * per_leaf : (k + 1) * per_leaf, :]
        for n in range(0, nbr_count, 2):
            near = [neighbours_ref[0, n + i, first + k] for i in range(2)]
            points = [source_ref[pl.ds(pl.multiple_of(i * group, group), group), :] for i in near]
            points = jnp.concatenate(points, axis=1)
            dist_sq = jnp.dot(
                target, jnp.concatenate([points, points], axis=0), preferred_element_type=f32
            )
            inverse = lax.rsqrt(dist_sq)
            cube = (inverse * inverse * inverse).astype(bf16)
            cube_ref[k, :, n * per_leaf : (n + 2) * per_leaf] = cube
    for k in range(count):
        near = [neighbours_ref[0, n, first + k] for n in range(nbr_count)]
        weights = [weight_ref[pl.ds(pl.multiple_of(i * deep, group), deep), :] for i in near]
        total = lax.dot_general(
            cube_ref[k],
            jnp.concatenate(weights, axis=1),
            (((1,), (1,)), ((), ())),
            preferred_element_type=f32,
        ).T
        total = sum(total[i * group : (i + 1) * group] for i in range(pieces))
        sums_ref[pl.ds(k, group, stride=count), :] = total

    got = [sums_ref[row * count : (row + 1) * count, :] for row in range(15)]
    start, mixed, rest = got[:3], [got[3 + 3 * i : 6 + 3 * i] for i in range(3)], got[12:]
    place = [sum(split(own_ref[axis, first : first + count, :], 2)) for axis in range(3)]
    norm = dot3(place, place)
    factor = live * inv_eight_pi
    shift = dot3(place, start) - (mixed[0][0] + mixed[1][1] + mixed[2][2])
    for i in range(3):
        turned = dot3(place, [2.0 * mixed[i][j] + mixed[j][i] for j in range(3)])
        out_ref[i] = (norm * start[i] + place[i] * shift - turned + rest[i]) * factor


def far_field(sources_ref, rows_ref, tile_of, out_ref, out_hbm, pick_ref, moved_ref, out_sem):
    coeffs, slot_count = out_ref.shape[0], rows_ref.shape[0]
    directions = pick_ref.shape[0] // slot_count
    tile = moved_ref.shape[1]
    octant = rows_ref[:, coeffs : coeffs + 2].astype(f32).astype(jnp.int32)
    octant = octant[:, :1] * id_base + octant[:, 1:]
    for t in range(directions):
        hit = octant == sources_ref[0, t : t + 1, :]
        pick_ref[t * slot_count : (t + 1) * slot_count, :] = jnp.where(hit, 1.0, 0.0).astype(bf16)
    rows = rows_ref[:, :coeffs]
    stores = []
    for i, start in enumerate(range(0, coeffs, tile)):
        ops_ref = tile_of(i)
        size = min(tile, coeffs - start)
        for t in range(directions):
            moved = jnp.dot(rows, ops_ref[t], preferred_element_type=f32)
            moved_ref[t * slot_count : (t + 1) * slot_count, :size] = moved.astype(bf16)
        for low in range(0, size, 2 * lanes):
            rest = min(2 * lanes, size - low)
            total = lax.dot_general(
                moved_ref[:, low : low + rest],
                pick_ref[...],
                (((0,), (0,)), ((), ())),
                preferred_element_type=f32,
            )
            at = pl.ds(start + low, rest)
            out_ref[at, :] = total.astype(bf16)
            sem = out_sem.at[len(stores)]
            stores.append(pltpu.make_async_copy(out_ref.at[at, :], out_hbm.at[at, :], sem))
            stores[-1].start()
    return stores


def near_kernel(
    slab_axis, neighbours_ref, live_ref, own_ref, odd_ref, even_ref, ops_hbm,
    early_ref, head_ref,
    point_ref, moment_ref, target_wide_ref, source_ref, weight_ref, target_ref, cube_ref, sums_ref, sem,
):
    at = (slice(None), pl.ds(0, head_ref.shape[1]), pl.ds(0, head_ref.shape[2]))
    head = pltpu.make_async_copy(ops_hbm.at[at], head_ref, sem)
    head.start()
    near_tables(
        slab_axis, own_ref, even_ref, odd_ref,
        point_ref, moment_ref, target_wide_ref, source_ref, weight_ref,
    )
    count = early_ref.shape[1]
    near_leaves(
        0, neighbours_ref, own_ref, live_ref[:count, :], target_wide_ref,
        source_ref, weight_ref, target_ref, cube_ref, sums_ref, early_ref,
    )
    early_ref[3] = live_ref[count:, :]
    head.wait()


def far_kernel(
    slab_axis, neighbours_ref, own_ref, odd_ref, even_ref, picks_ref, rows_ref, head_ref, early_ref,
    ops_hbm, local_hbm, velocity_hbm,
    point_ref, moment_ref, target_wide_ref, source_ref, weight_ref, target_ref, cube_ref, sums_ref,
    ops_ref, pick_ref, moved_ref, local_ref, late_ref, velocity_ref, ops_sem, out_sem,
):
    coeffs, tile = ops_hbm.shape[1], moved_ref.shape[1]
    loads = [None]
    for i, start in enumerate(range(tile, coeffs, tile)):
        at = pl.ds(start, min(tile, coeffs - start))
        loads.append(pltpu.make_async_copy(ops_hbm.at[:, :, at], ops_ref.at[:, :, at], ops_sem.at[i + 1]))
        loads[-1].start()

    count = early_ref.shape[1]
    near_tables(
        slab_axis, own_ref, even_ref, odd_ref,
        point_ref, moment_ref, target_wide_ref, source_ref, weight_ref,
    )
    near_leaves(
        count, neighbours_ref, own_ref, early_ref[3], target_wide_ref,
        source_ref, weight_ref, target_ref, cube_ref, sums_ref, late_ref,
    )
    for axis in range(3):
        velocity_ref[axis, :count, :] = early_ref[axis]
        velocity_ref[axis, count:, :] = late_ref[axis]
    velocity_store = pltpu.make_async_copy(velocity_ref, velocity_hbm, ops_sem.at[len(loads)])
    velocity_store.start()

    def tile_of(i):
        if i == 0:
            return head_ref
        loads[i].wait()
        return ops_ref.at[:, :, pl.ds(i * tile, min(tile, coeffs - i * tile))]

    stores = far_field(picks_ref, rows_ref, tile_of, local_ref, local_hbm, pick_ref, moved_ref, out_sem)
    for store in stores + [velocity_store]:
        store.wait()


def vmem():
    return pl.BlockSpec(memory_space=pltpu.VMEM)


def in_hbm(array):
    return pltpu.with_memory_space_constraint(array, pltpu.HBM)


def smem():
    return pl.BlockSpec(memory_space=pltpu.SMEM)


def hbm():
    return pl.BlockSpec(memory_space=pltpu.HBM)


def near_scratch(neighbours, packed):
    _, leaves, per_leaf = packed.shape
    table, count = 3 * leaves, leaves // 2
    return [
        pltpu.VMEM((table * group, per_leaf), f32),
        pltpu.VMEM((table * group, per_leaf), f32),
        pltpu.VMEM((leaves * 2 * group, per_leaf), f32),
        pltpu.VMEM((table * group, per_leaf), bf16),
        pltpu.VMEM((table * pieces * group, per_leaf), bf16),
        pltpu.VMEM((count * per_leaf, 2 * group), bf16),
        pltpu.VMEM((count, per_leaf, neighbours.shape[1] * per_leaf), bf16),
        pltpu.VMEM((group * count, per_leaf), f32),
    ]


def call_near(neighbours, live, packed, odd, even, m2l_ops, tile):
    _, leaves, per_leaf = packed.shape
    directions, coeffs, _ = m2l_ops.shape
    return pl.pallas_call(
        functools.partial(near_kernel, "nb"),
        out_shape=(
            pltpu.VMEM((4, leaves // 2, per_leaf), f32),
            pltpu.VMEM((directions, coeffs, tile), bf16),
        ),
        in_specs=[smem()] + [vmem()] * 4 + [hbm()],
        out_specs=(vmem(), vmem()),
        scratch_shapes=near_scratch(neighbours, packed) + [pltpu.SemaphoreType.DMA],
        compiler_params=pltpu.CompilerParams(vmem_limit_bytes=24 * 2**20),
        name="near",
    )(neighbours, live, packed, odd, even, in_hbm(m2l_ops))


def call_far(neighbours, packed, odd, even, m2l_sources, arrived, head, early, m2l_ops):
    _, leaves, per_leaf = packed.shape
    directions, coeffs, _ = m2l_ops.shape
    tile = head.shape[2]
    owned = m2l_sources.shape[2]
    picks = directions * arrived.shape[0]
    steps = -(-coeffs // tile)
    return pl.pallas_call(
        functools.partial(far_kernel, "nb"),
        out_shape=(
            jax.ShapeDtypeStruct((coeffs, owned), bf16),
            jax.ShapeDtypeStruct((3, leaves, per_leaf), f32),
        ),
        in_specs=[smem()] + [vmem()] * 7 + [hbm()],
        out_specs=(hbm(), hbm()),
        scratch_shapes=near_scratch(neighbours, packed)
        + [
            pltpu.VMEM(m2l_ops.shape, bf16),
            pltpu.VMEM((picks, owned), bf16),
            pltpu.VMEM((picks, tile), bf16),
            pltpu.VMEM((coeffs, owned), bf16),
            pltpu.VMEM((3, leaves - leaves // 2, per_leaf), f32),
            pltpu.VMEM((3, leaves, per_leaf), f32),
            pltpu.SemaphoreType.DMA((steps + 1,)),
            pltpu.SemaphoreType.DMA((2 * steps,)),
        ],
        compiler_params=pltpu.CompilerParams(vmem_limit_bytes=40 * 2**20),
        name="far",
    )(neighbours, packed, odd, even, m2l_sources, arrived, head, early, in_hbm(m2l_ops))


def call_presum(hx_count, partial_multipoles, shared_slots, positions, forces, leaf_counts, neighbours):
    row_count, coeffs = partial_multipoles.shape[1:]
    cap = row_count // hx_count
    uniq = cap // 4
    slot_count = hx_count * uniq
    width = -(-(coeffs + 2) // lanes) * lanes
    tile = width
    steps = -(-coeffs // tile)
    leaves = leaf_counts.shape[1]
    per_leaf = positions.shape[2] // leaves

    return pl.pallas_call(
        functools.partial(presum_kernel, cap, uniq, tile),
        out_shape=(
            jax.ShapeDtypeStruct((slot_count, width), bf16),
            pltpu.VMEM((6, leaves, per_leaf), f32),
            pltpu.VMEM((9, leaves, per_leaf), bf16),
            pltpu.VMEM((leaves, per_leaf), f32),
            pltpu.SMEM(neighbours.shape, jnp.int32),
        ),
        in_specs=[hbm()] * 6,
        out_specs=(hbm(), vmem(), vmem(), vmem(), smem()),
        scratch_shapes=[
            pltpu.VMEM(leaf_counts.shape, jnp.int32),
            pltpu.VMEM(shared_slots.shape, jnp.int32),
            pltpu.VMEM((coeffs, row_count), bf16),
            pltpu.VMEM((3, leaves, per_leaf), f32),
            pltpu.VMEM((3, leaves, per_leaf), f32),
            pltpu.VMEM((slot_count, width), bf16),
            pltpu.SemaphoreType.DMA((5,)),
            pltpu.SemaphoreType.DMA((steps,)),
            pltpu.SemaphoreType.DMA((steps,)),
        ],
        compiler_params=pltpu.CompilerParams(vmem_limit_bytes=16 * 2**20),
        name="presum",
    )(
        *map(
            in_hbm,
            (
                leaf_counts,
                shared_slots,
                partial_multipoles[0].T,
                positions[0].reshape(3, leaves, per_leaf),
                forces[0].reshape(3, leaves, per_leaf),
                neighbours,
            ),
        )
    )


def on_device(
    partial_multipoles,
    shared_slots,
    m2l_sources,
    m2l_ops,
    positions,
    forces,
    leaf_counts,
    neighbours,
):
    hx_count, nb_count = lax.axis_size("hx"), lax.axis_size("nb")
    sums, packed, sent, live, sources = call_presum(
        hx_count, partial_multipoles, shared_slots, positions, forces, leaf_counts, neighbours
    )

    even_pairs = [(i, i + 1) for i in range(0, nb_count - 1, 2)]
    odd_pairs = [(i, i + 1) for i in range(1, nb_count - 1, 2)]
    even = lax.ppermute(sent, "nb", even_pairs + [(j, i) for i, j in even_pairs])
    odd = lax.ppermute(sent, "nb", odd_pairs + [(j, i) for i, j in odd_pairs])
    arrived = lax.all_to_all(
        sums.reshape(hx_count, -1, sums.shape[1]), "hx", split_axis=0, concat_axis=0, tiled=True
    ).reshape(sums.shape)

    early, head = call_near(sources, live, packed, odd, even, m2l_ops, 4 * lanes)
    local, velocity = call_far(
        sources, packed, odd, even, m2l_sources, arrived, head, early, m2l_ops
    )

    return local.T[None], velocity.reshape(positions.shape)


def solution(mesh):
    placed = (
        P("nb", "hx", None),
        P("nb", "hx"),
        P("nb", None, "hx"),
        P(),
        P("nb", None, "hx"),
        P("nb", None, "hx"),
        P("nb", "hx"),
        P("nb", None, "hx"),
    )
    return jax.shard_map(
        on_device,
        mesh=mesh,
        in_specs=placed,
        out_specs=(P("nb", "hx", None), P("nb", None, "hx")),
        check_vma=False,
    )
```
